512 devices in a mesh: date: 64 (over z, x, core), space: 8 (over y).
Axes of the slice: x: 4, y: 8, z: 8, core: 2. Of those that a mesh axis runs over, the one named last changes fastest.
Arguments:
- chips: bfloat16 [1024, 8, 4096], P('date', 'space'), may hold values from -150 to 150
- pair_target: int32 [4096, 1], P('date'), may hold values from 0 to 63; in each aligned block of 64 rows (0 to 63, 64 to 127, ...) at most 2 rows name the same one
- pair_slot: int32 [4096], P('date'), may hold values from 0 to 15
- offset_fix: int32 [4096, 8, 2], P('date', 'space'), may hold values from -192 to 192
Outputs:
- displacement: float32 [2, 1024, 8], P(None, 'date', 'space')
- pair_measure: float32 [3, 4096, 8], P(None, 'date', 'space')
The draws below stay inside these ranges and needn't reach their ends.
Inputs may be any that keep to these rules, and one draw needn't show every extreme that they name: `pair_target`: in the 64 rows of one index of date, no value is named more than 2 times, and in some of those blocks a value is named exactly 2 times.
All inputs are finite; a program needn't handle non-finite values.
Results may differ from the reference program's by a relative error of at most 0.0015.
Values may be sent and summed in bfloat16 or wider, within the bound.
A program may use at most 64 MiB of HBM per device.

```python
import math
import jax
import jax.numpy as jnp
import numpy as np
from jax import lax

CHIP = 64
DATE_DEV = 16
LINKS = 4
PAIR_DEV = 64
CAP = 2
DATES = 1024
CHIPS = 8
PAIRS = 4096
N_DATE = 64


def draw_chips(key, part):
    key = jax.random.fold_in(key, 11)
    key_noise, key_scale, key_rows = jax.random.split(key, 3)
    noise = jnp.clip(jax.random.normal(key_noise, (DATES, CHIPS, CHIP, CHIP), jnp.float32), -5.0, 5.0)
    chip_scale = jnp.exp(jax.random.uniform(key_scale, (DATES, CHIPS, 1, 1), jnp.float32, 0.0, math.log(10.0)))
    row_scale = jnp.exp(jax.random.uniform(key_rows, (DATES, CHIPS, CHIP, 1), jnp.float32, 0.0, math.log(3.0)))
    return (noise * chip_scale * row_scale).reshape(DATES, CHIPS, CHIP * CHIP).astype(jnp.bfloat16)


def touch_ends(entries, own_key, low, largest):
    spot = [jax.random.randint(jax.random.fold_in(own_key, axis), (), 0, length) for axis, length in enumerate(entries.shape)]
    main_axis = entries.shape.index(max(entries.shape))
    beside = spot[:main_axis] + [(spot[main_axis] + 1) % entries.shape[main_axis]] + spot[main_axis + 1:]
    return entries.at[tuple(spot)].set(low).at[tuple(beside)].set(largest)


def deal_out(rng, own, number, rows, count, top, reach, slope):
    sequence = jax.random.permutation(rng, count)
    crowded, common = shares(count, rows * top, reach, slope, True), shares(count, rows * top, reach, slope, False)
    places = jnp.arange(count)

    def named(sizes, turn):
        used = int((sizes > 0).sum())
        fixed = max(1, used // 4)
        shifted = fixed + (places - fixed + turn * (used - fixed)) % max(1, count - fixed)
        return jnp.zeros((count,), jnp.int32).at[sequence[jnp.where(places < fixed, places, shifted)]].set(jnp.asarray(sizes, jnp.int32))

    sizes = jnp.where(number % 4 == 0, named(crowded, number // 4), named(common, number - number // 4 - 1))
    mixed = jax.random.permutation(jax.random.fold_in(own, 3), count)
    donor, sink = mixed[0:count // 2 * 2:2], mixed[1:count // 2 * 2:2]
    slack = jnp.minimum(sizes[donor] - 1, reach - sizes[sink]) // 2
    slack = jnp.where((donor == sequence[0]) | (sink == sequence[0]) | (sizes[sink] == 0), 0, jnp.maximum(slack, 0))
    shifted = jax.random.randint(jax.random.fold_in(own, 4), (count // 2,), 0, 1 << 20) % (slack + 1)
    sizes = sizes.at[donor].add(-shifted).at[sink].add(shifted)
    labels = jnp.searchsorted(jnp.cumsum(sizes), jnp.arange(rows * top), side="right").astype(jnp.int32)
    listing = labels.reshape(top, rows).T
    listing = listing[jax.random.permutation(jax.random.fold_in(own, 1), rows)]
    turn = jax.random.randint(jax.random.fold_in(own, 2), (rows, 1), 0, top)
    return jnp.take_along_axis(listing, (jnp.arange(top)[None, :] + turn) % top, axis=1)


def shares(count, total, reach, lean, full):
    portions = [(1 << 20) // math.isqrt(grade ** lean) + 1 for grade in range(1, count + 1)]
    largest = reach if full else min(reach, max(-(-total // count), total * portions[0] // sum(portions)))
    least = 1 if total - largest >= count - 1 else 0
    given, surplus = [largest] + [least] * (count - 1), total - largest - least * (count - 1)
    while surplus > 0:
        movable = [i for i in range(1, count) if given[i] < largest] or [i for i in range(1, count) if given[i] < reach]
        pool, budget = sum([portions[i] for i in movable]), surplus
        for i in movable:
            extra = min(reach - given[i], max(1, budget * portions[i] // pool), surplus)
            given[i] = given[i] + extra
            surplus = surplus - extra
    return np.array(given)


def setup_inputs(seed: int = 0) -> dict:
    key_of = jax.random.split(jax.random.key(seed), 5)
    chips = draw_chips(jax.random.fold_in(key_of[4], 71), 0)
    pair_target_keys = jax.random.split(jax.random.fold_in(key_of[1], 1), PAIRS // PAIR_DEV)
    pair_target_turns = jax.random.permutation(jax.random.fold_in(key_of[1], 3), PAIRS // PAIR_DEV)
    pair_target = jax.vmap(lambda own, number: deal_out(jax.random.fold_in(key_of[1], 2), own, number, PAIR_DEV, N_DATE, 1, CAP, 2))(pair_target_keys, pair_target_turns).reshape((PAIRS, 1))
    pair_slot = touch_ends(jax.random.randint(key_of[2], (PAIRS,), 0, DATE_DEV), jax.random.fold_in(key_of[2], 1), 0, DATE_DEV - 1).astype(jnp.int32)
    offset_fix = touch_ends(jax.random.randint(key_of[3], (PAIRS, CHIPS, 2), -192, 193), jax.random.fold_in(key_of[3], 1), -192, 192).astype(jnp.int32)
    return dict(chips=chips, pair_target=pair_target, pair_slot=pair_slot, offset_fix=offset_fix)


SIGMA = 0.6
STEP = 1.0
ZSCALE = 0.5
EPS = 1e-06
LAMBDA = 2.0
MUS = (4.0, 2.0, 1.0)
FIXED = 32.0

def kernels(shifts):
    positions = jnp.arange(CHIP, dtype=jnp.float32)
    spacing = positions[:, None] - positions[None, :]
    distance = spacing - shifts[..., None, None]
    return jnp.exp(-(distance * distance) / (2.0 * SIGMA * SIGMA)).astype(jnp.bfloat16)

def correlate(first, second, offsets):
    levels = STEP * (jnp.arange(3, dtype=jnp.float32) - 1.0)
    shifts = offsets[:, :, None] + levels
    kernel_y = lax.optimization_barrier(kernels(shifts[:, 0])).astype(jnp.float32)
    kernel_x = lax.optimization_barrier(kernels(shifts[:, 1])).astype(jnp.float32)
    first_mat = first.reshape(-1, CHIP, CHIP).astype(jnp.float32)
    second_mat = second.reshape(-1, CHIP, CHIP).astype(jnp.float32)
    moved = jnp.einsum('qak,qxnk->qxan', first_mat, kernel_x)
    moved = lax.optimization_barrier(moved.astype(jnp.bfloat16)).astype(jnp.float32)
    lifted = jnp.einsum('qymk,qmn->qykn', kernel_y, second_mat)
    lifted = lax.optimization_barrier(lifted.astype(jnp.bfloat16)).astype(jnp.float32)
    inner = jnp.einsum('qykn,qxkn->qyx', lifted, moved)
    first_norm = lax.optimization_barrier(jnp.sum(first_mat * first_mat, axis=(1, 2)))
    second_norm = lax.optimization_barrier(jnp.sum(second_mat * second_mat, axis=(1, 2)))
    scores = CHIP * inner / jnp.sqrt((first_norm + EPS) * (second_norm + EPS))[:, None, None]
    raised = jnp.exp(ZSCALE * scores)
    weights = raised / lax.optimization_barrier(jnp.sum(raised, axis=(1, 2), keepdims=True))
    move_y = offsets[:, 0] + lax.optimization_barrier(jnp.sum(lax.optimization_barrier(jnp.sum(weights, axis=2)) * levels, axis=1))
    move_x = offsets[:, 1] + lax.optimization_barrier(jnp.sum(lax.optimization_barrier(jnp.sum(weights, axis=1)) * levels, axis=1))
    quality = jax.nn.sigmoid(ZSCALE * lax.optimization_barrier(jnp.sum(weights * scores, axis=(1, 2))))
    return jnp.stack([move_y, move_x, quality], axis=1)

def reference(chips, pair_target, pair_slot, offset_fix):
    first_date = jnp.arange(PAIRS, dtype=jnp.int32) // LINKS
    second_date = (pair_target[:, 0] * DATE_DEV + pair_slot).astype(jnp.int32)
    offsets = offset_fix.astype(jnp.float32) / FIXED

    def block_measure(packed):
        first_rows, second_rows, offset_rows = packed
        first = chips[first_rows].reshape(-1, CHIP * CHIP)
        second = chips[second_rows].reshape(-1, CHIP * CHIP)
        return correlate(first, second, offset_rows.reshape(-1, 2)).reshape(16, CHIPS, 3)
    measured = lax.map(block_measure, (first_date.reshape(-1, 16), second_date.reshape(-1, 16), offsets.reshape(-1, 16, CHIPS, 2)))
    measured = measured.reshape(PAIRS, CHIPS, 3)
    measure = jnp.transpose(measured[:, :, :2], (0, 2, 1))
    quality = measured[:, :, 2]
    field = jnp.zeros((DATES, 2, CHIPS), jnp.float32)
    for scale in MUS:
        first_val = field[first_date]
        second_val = field[second_date]
        resid = measure - (second_val - first_val)
        spread = scale * scale
        weight = quality * spread / (spread + lax.optimization_barrier(jnp.sum(resid * resid, axis=1)))
        to_second = jnp.concatenate([weight[:, None] * (first_val + measure), weight[:, None]], axis=1)
        to_first = jnp.concatenate([weight[:, None] * (second_val - measure), weight[:, None]], axis=1)
        totals = jax.ops.segment_sum(to_second, second_date, DATES) + jax.ops.segment_sum(to_first, first_date, DATES)
        padded = jnp.pad(field, ((0, 0), (0, 0), (1, 1)))
        beside = padded[:, :, :-2] + padded[:, :, 2:]
        field = (LAMBDA * beside + totals[:, :2]) / (2.0 * LAMBDA + totals[:, 2:3])
    return (jnp.transpose(field, (1, 0, 2)), jnp.transpose(measured, (2, 0, 1)))
```

```python
import jax
import jax.numpy as jnp
from jax import lax
from jax.experimental import pallas as pl
from jax.experimental.pallas import tpu as pltpu
from jax.sharding import PartitionSpec as P

CHIP = 64
LINKS = 4
ROW = 8
NZ = 8
DATE_DEV = 16
PAIRS = 64
HALF = 8
SIGMA = 0.6
ZSCALE = 0.5
EPS = 1e-06
LAMBDA = 2.0
MUS = (4.0, 2.0, 1.0)
FIXED = 32.0
ITEMS = 11
F32 = jnp.float32
BF16 = jnp.bfloat16
PRE = (16, 16, 16, 16)


def iota(shape, dim):
    return lax.broadcasted_iota(jnp.int32, shape, dim)


def fold(rows):
    return jnp.sum(rows.reshape(rows.shape[0] // 8, 8, 128), axis=0)


def split_bf16(value):
    high = value.astype(BF16)
    return high, (value - high.astype(F32)).astype(BF16)


def kernel(
    chips,
    target,
    slot,
    offs_s,
    offs_v,
    measure_out,
    disp_out,
    tmp,
    held0,
    held1,
    held2,
    held3,
    held4,
    held5,
    held6,
    held7,
    xsend,
    recv,
    bnorm,
    rowx,
    zsec,
    reqv,
    req,
    mbuf,
    lhs,
    onehot,
    member,
    sums,
    mrow,
    mall,
    spread,
    fsend,
    halo,
    sem_req,
    row_s,
    row_r,
    zsec_s,
    zsec_r,
    plus_s,
    plus_r,
    minus_s,
    minus_r,
    x_s,
    x_r,
    mrow_s,
    mrow_r,
    mall_s,
    mall_r,
    halo_s,
    halo_r,
):
    held = (held0, held1, held2, held3, held4, held5, held6, held7)
    date = lax.axis_index("date")
    y = lax.axis_index("space")
    ny = lax.axis_size("space")
    mz = lax.div(date, ROW)
    me = lax.rem(date, ROW)

    def row_peer(k):
        return {"date": mz * ROW + lax.rem(me + k, ROW)}

    def z_peer(k):
        return {"date": lax.rem(mz + k, NZ) * ROW + me}

    def y_peer(k):
        return {"space": lax.rem(y + k, ny)}

    def remote(src, dst, ssem, rsem, peer):
        return pltpu.make_async_remote_copy(
            src_ref=src,
            dst_ref=dst,
            send_sem=ssem,
            recv_sem=rsem,
            device_id=peer,
            device_id_type=pl.DeviceIdType.MESH,
        )

    barrier = pltpu.get_barrier_semaphore()
    for k in range(1, ROW):
        pl.semaphore_signal(barrier, inc=1, device_id=row_peer(k), device_id_type=pl.DeviceIdType.MESH)
    for k in range(1, NZ):
        pl.semaphore_signal(barrier, inc=1, device_id=z_peer(k), device_id_type=pl.DeviceIdType.MESH)
    for k in (1, ny - 1):
        pl.semaphore_signal(barrier, inc=1, device_id=y_peer(k), device_id_type=pl.DeviceIdType.MESH)

    for j in range(32):
        tmp[pl.ds(j, DATE_DEV, stride=32), :] = chips[:, 128 * j : 128 * j + 128].astype(F32)
    for d in range(DATE_DEV):
        own = tmp[pl.ds(32 * d, 32), :]
        held[0][d] = own.astype(BF16)
        bnorm[pl.ds(8 * d, 8), :] = fold(own * own)

    sub = iota((PAIRS, 128), 0)
    lane = iota((PAIRS, 128), 1)
    zeros64 = jnp.zeros((1, 128 - PAIRS), jnp.int32)
    trow = jnp.concatenate([target[...], zeros64 - 1], axis=1).astype(F32)
    srow = jnp.concatenate([slot[...], zeros64], axis=1).astype(F32)
    tb = jnp.broadcast_to(trow, (PAIRS, 128))
    sb = jnp.broadcast_to(srow, (PAIRS, 128))
    eye = sub == lane
    tcol = jnp.sum(jnp.where(eye, tb, 0.0), axis=1, keepdims=True)
    scol = jnp.sum(jnp.where(eye, sb, 0.0), axis=1, keepdims=True)
    twin = jnp.where((tcol == tb) & (lane < sub), 1.0, 0.0)
    place = 2.0 * tcol + jnp.sum(twin, axis=1, keepdims=True)
    wanted = jnp.sum(jnp.where(lane.astype(F32) == place, scol, 0.0), axis=0, keepdims=True)
    place_row = jnp.sum(jnp.where(eye, place, 0.0), axis=0, keepdims=True)
    deal = jnp.where(lane == me * DATE_DEV + sub // LINKS, 1.0, 0.0).astype(BF16)
    r8 = iota((8, PAIRS), 0)
    l8 = iota((8, PAIRS), 1)
    ours = (l8 % LINKS) == (r8 % LINKS)
    named = jnp.where(r8 < 4, jnp.broadcast_to(trow[:, :PAIRS], (8, PAIRS)), jnp.broadcast_to(srow[:, :PAIRS], (8, PAIRS)))
    named = jnp.where(ours, named, 0.0).astype(BF16)
    rowx[pl.ds(0, 8), :] = jnp.dot(named, deal, preferred_element_type=F32)
    rowx[pl.ds(8, 8), :] = jnp.broadcast_to(wanted, (8, 128))

    pl.semaphore_wait(barrier, ROW - 1 + NZ - 1 + 2)

    def row_copy(k):
        return remote(rowx.at[pl.ds(0, 16)], rowx.at[pl.ds(16 * k, 16)], row_s.at[k], row_r.at[k], row_peer(k))

    def ring_part(t, half):
        return held[t].at[pl.ds(half * HALF, HALF)]

    def plus_copy(s, half):
        return remote(
            ring_part(max(2 * s - 3, 0), half),
            ring_part(2 * s - 1, half),
            plus_s.at[s - 1, half],
            plus_r.at[s - 1, half],
            z_peer(1),
        )

    def minus_copy(s, half):
        return remote(
            ring_part(2 * s - 2, half),
            ring_part(min(2 * s, 7), half),
            minus_s.at[s - 1, half],
            minus_r.at[s - 1, half],
            z_peer(NZ - 1),
        )

    def plus_arrived(s, half):
        plus_copy(s, half).wait_recv()

    def minus_arrived(s, half):
        minus_copy(s, half).wait_recv()

    for k in range(1, ROW):
        row_copy(k).start()
    for half in (0, 1):
        plus_copy(1, half).start()
        minus_copy(1, half).start()
    for k in range(1, ROW):
        row_copy(k).wait_recv()

    reqv[pl.ds(0, 8), :] = rowx[pl.ds(8, 8, stride=16), :].astype(jnp.int32)
    reqv[pl.ds(8, 8), :] = jnp.broadcast_to(place_row, (8, 128)).astype(jnp.int32)
    fetch = pltpu.make_async_copy(reqv, req, sem_req)
    fetch.start()
    total = rowx[pl.ds(0, 8), :]
    for k in range(1, ROW):
        total = total + rowx[pl.ds(16 * k, 8), :]
    zsec[pl.ds(8 * mz, 8), :] = total

    def zsec_copy(k):
        mine = zsec.at[pl.ds(8 * mz, 8)]
        return remote(mine, mine, zsec_s.at[k], zsec_r.at[k], z_peer(k))

    def zsec_arrived(k):
        theirs = zsec.at[pl.ds(8 * lax.rem(mz - k + NZ, NZ), 8)]
        remote(theirs, theirs, zsec_s.at[k], zsec_r.at[k], z_peer(k)).wait_recv()

    for k in range(1, NZ):
        zsec_copy(k).start()
    fetch.wait()

    def x_copy(t, k, block):
        return remote(
            xsend.at[pl.ds((t * ROW + k) * 2, 2)],
            recv.at[pl.ds(block * 16 + me * 2, 2)],
            x_s.at[t, k],
            x_r.at[t, k],
            row_peer(k),
        )

    def x_arrived(t, k, block):
        theirs = recv.at[pl.ds(block * 16 + lax.rem(me - k + ROW, ROW) * 2, 2)]
        remote(xsend.at[pl.ds((t * ROW + k) * 2, 2)], theirs, x_s.at[t, k], x_r.at[t, k], row_peer(k)).wait_recv()

    def block_of(t):
        step = (t + 1) // 2
        return lax.rem(mz - step + NZ, NZ) if t % 2 else lax.rem(mz + step, NZ)

    def serve(t):
        block = block_of(t)
        for k in (1, 7, 2, 6, 3, 5, 4, 0):
            asker = (ROW - k) % ROW
            for r in (0, 1):
                chip = held[t][jnp.clip(req[asker, block * 16 + me * 2 + r], 0, DATE_DEV - 1)]
                if k:
                    xsend[(t * ROW + k) * 2 + r] = chip
                else:
                    recv[block * 16 + me * 2 + r] = chip
            if k:
                x_copy(t, k, block).start()

    lane64 = iota((CHIP, 128), 1)
    spacing_x = ((lane64 % CHIP) - iota((CHIP, 128), 0)).astype(F32)
    left64 = lane64 < CHIP
    lane32 = iota((32, 128), 1)
    q32 = lane32 % CHIP
    m32 = 2 * (q32 % 32) + q32 // 32
    spacing_y = (m32 - 2 * iota((32, 128), 0) - lane32 // CHIP).astype(F32)
    left32 = lane32 < CHIP
    decay = -1.0 / (2.0 * SIGMA * SIGMA)

    def prepare(i, carry):
        off_y = offs_s[0, i].astype(F32) * (1.0 / FIXED)
        off_x = offs_s[1, i].astype(F32) * (1.0 / FIXED)
        tops, bottoms = [], []
        for level in (-1.0, 0.0, 1.0):
            gap = spacing_x - (off_x + level)
            bell = jnp.exp(gap * gap * decay)
            tops.append(jnp.where(left64, bell, 0.0).astype(BF16))
            bottoms.append(jnp.where(left64, 0.0, bell).astype(BF16))
        wide = jnp.concatenate([jnp.concatenate(tops, axis=1), jnp.concatenate(bottoms, axis=1)], axis=0)
        own = held[0][lax.div(i, LINKS)]
        mbuf[i] = jnp.dot(own, wide, preferred_element_type=F32).astype(BF16)
        for e, level in enumerate((-1.0, 0.0, 1.0)):
            gap = spacing_y - (off_y + level)
            lhs[i, pl.ds(32 * e, 32), :] = jnp.exp(gap * gap * decay).astype(BF16)
        return carry

    def prepare_part(n):
        low = sum(PRE[:n])
        lax.fori_loop(low, low + PRE[n], prepare, 0)

    serve(0)
    prepare_part(0)
    for s in (1, 2, 3):
        for half in (0, 1):
            plus_arrived(s, half)
            if s < 3 or half == 0:
                plus_copy(s + 1, half).start()
            minus_arrived(s, half)
            if s < 3 or half == 1:
                minus_copy(s + 1, half).start()
        serve(2 * s - 1)
        serve(2 * s)
        prepare_part(s)
    for k in range(1, NZ):
        zsec_arrived(k)

    later = []
    for l in range(LINKS):
        dev = zsec[pl.ds(l, NZ, stride=8), :].astype(jnp.int32)
        pos = zsec[pl.ds(4 + l, NZ, stride=8), :].astype(jnp.int32)
        later.append((dev // ROW, (dev % ROW) * DATE_DEV + pos))
    down128 = iota((128, 128), 0)
    down8 = iota((8, 128), 0)
    for l in range(LINKS):
        for z in range(NZ):
            c = l * NZ + z
            hit = jnp.broadcast_to(later[l][1][z : z + 1, :], (128, 128)) == down128
            onehot[:, pl.ds(128 * c, 128)] = jnp.where(hit, 1.0, 0.0).astype(BF16)
            hit = jnp.broadcast_to(later[l][0][z : z + 1, :], (8, 128)) == down8
            member[pl.ds(8 * c, 8), :] = jnp.where(hit, 1.0, 0.0)

    plus_arrived(4, 0)
    minus_arrived(4, 1)
    serve(7)
    for t in range(NZ):
        for k in range(1, ROW):
            x_arrived(t, k, block_of(t))

    def score(i, carry):
        chip = recv[jnp.clip(req[8, i], 0, NZ * ROW * 2 - 1)].astype(F32)
        swapped = pltpu.roll(chip, CHIP, 1)
        blocks = jnp.concatenate(
            [
                jnp.where(left32, chip, 0.0).astype(BF16),
                jnp.where(left32, swapped, 0.0).astype(BF16),
                jnp.where(left32, 0.0, swapped).astype(BF16),
                jnp.where(left32, 0.0, chip).astype(BF16),
            ],
            axis=0,
        )
        lifted = jnp.dot(lhs[i], blocks, preferred_element_type=F32).astype(BF16).astype(F32)
        moved = mbuf[i].astype(F32)
        for ky in range(3):
            for kx in range(3):
                part = fold(lifted[32 * ky : 32 * ky + 32] * moved[:, 128 * kx : 128 * kx + 128])
                sums[pl.ds((3 * ky + kx) * PAIRS + i, 8, stride=ITEMS * PAIRS), :] = part
        sums[pl.ds(9 * PAIRS + i, 8, stride=ITEMS * PAIRS), :] = fold(chip * chip)
        sums[pl.ds(10 * PAIRS + i, 8, stride=ITEMS * PAIRS), :] = bnorm[pl.ds(8 * lax.div(i, LINKS), 8), :]
        return carry

    lax.fori_loop(0, PAIRS, score, 0)

    rows = []
    for item in range(ITEMS):
        part = sums[pl.ds(item * PAIRS, PAIRS), :]
        for s in range(1, 8):
            part = part + sums[pl.ds(s * ITEMS * PAIRS + item * PAIRS, PAIRS), :]
        rows.append(jnp.sum(part.T, axis=0, keepdims=True))
    size = CHIP / jnp.sqrt((rows[10] + EPS) * (rows[9] + EPS))
    scores = [rows[q] * size for q in range(9)]
    raised = [jnp.exp(ZSCALE * s) for s in scores]
    whole = raised[0]
    for q in range(1, 9):
        whole = whole + raised[q]
    weights = [r / whole for r in raised]
    offs = offs_v[...].astype(F32) * (1.0 / FIXED)
    move_y = offs[0:1] + ((weights[6] + weights[7] + weights[8]) - (weights[0] + weights[1] + weights[2]))
    move_x = offs[1:2] + ((weights[2] + weights[5] + weights[8]) - (weights[0] + weights[3] + weights[6]))
    blend = weights[0] * scores[0]
    for q in range(1, 9):
        blend = blend + weights[q] * scores[q]
    quality = 1.0 / (1.0 + jnp.exp(-ZSCALE * blend))
    measure_out[0] = move_y
    measure_out[1] = move_x
    measure_out[2] = quality

    up = jnp.where(r8 < 4, jnp.broadcast_to(move_y, (8, PAIRS)), jnp.broadcast_to(move_x, (8, PAIRS)))
    up = jnp.where(ours, up, 0.0)
    down = jnp.where(ours & (r8 < 4), jnp.broadcast_to(quality, (8, PAIRS)), 0.0)
    both = jnp.concatenate([up, down], axis=0)
    first = both.astype(BF16)
    rest = both - first.astype(F32)
    second = rest.astype(BF16)
    third = (rest - second.astype(F32)).astype(BF16)
    dealt = jnp.dot(jnp.concatenate([first, second, third], axis=0), deal, preferred_element_type=F32)
    mrow[pl.ds(0, 16), :] = dealt[0:16] + dealt[16:32] + dealt[32:48]

    def mrow_copy(k):
        return remote(mrow.at[pl.ds(0, 16)], mrow.at[pl.ds(16 * k, 16)], mrow_s.at[k], mrow_r.at[k], row_peer(k))

    for k in range(1, ROW):
        mrow_copy(k).start()
    for k in range(1, ROW):
        mrow_copy(k).wait_recv()
    total = mrow[pl.ds(0, 16), :]
    for k in range(1, ROW):
        total = total + mrow[pl.ds(16 * k, 16), :]
    mall[pl.ds(16 * mz, 16), :] = total

    def mall_copy(k):
        mine = mall.at[pl.ds(16 * mz, 16)]
        return remote(mine, mine, mall_s.at[k], mall_r.at[k], z_peer(k))

    def mall_arrived(k):
        theirs = mall.at[pl.ds(16 * lax.rem(mz - k + NZ, NZ), 16)]
        remote(theirs, theirs, mall_s.at[k], mall_r.at[k], z_peer(k)).wait_recv()

    for k in range(1, NZ):
        mall_copy(k).start()
    for k in range(1, NZ):
        mall_arrived(k)

    meas = [[mall[pl.ds(4 * a + l, NZ, stride=16), :] for l in range(LINKS)] for a in range(2)]
    qual = [mall[pl.ds(8 + l, NZ, stride=16), :] for l in range(LINKS)]
    field = None

    def halo_copy(n, side):
        return remote(
            fsend.at[pl.ds(16 * n, 16)],
            halo.at[pl.ds(16 * (2 * n + side), 16)],
            halo_s.at[n, side],
            halo_r.at[n, side],
            y_peer(1 if side == 0 else ny - 1),
        )

    for n, scale in enumerate(MUS):
        square = scale * scale
        numer = [None, None]
        denom = None
        for l in range(LINKS):
            if field is None:
                here = [0.0, 0.0]
                there = [0.0, 0.0]
            else:
                here = field
                there = []
                for a in range(2):
                    got = None
                    for z in range(NZ):
                        table = jnp.broadcast_to(field[a][z : z + 1, :], (NZ, 128))
                        found = jnp.take_along_axis(table, later[l][1], axis=1, mode="promise_in_bounds")
                        got = found if got is None else jnp.where(later[l][0] == z, found, got)
                    there.append(got)
            resid = [meas[a][l] - (there[a] - here[a]) for a in range(2)]
            gnc = qual[l] * square / (square + (resid[0] * resid[0] + resid[1] * resid[1]))
            values = [gnc * (here[a] + meas[a][l]) for a in range(2)] + [gnc]
            for a in range(2):
                back = gnc * (there[a] - meas[a][l])
                numer[a] = back if l == 0 else numer[a] + back
            denom = gnc if l == 0 else denom + gnc
            for z in range(NZ):
                c = l * NZ + z
                mask = member[pl.ds(8 * c, 8), :]
                tall = jnp.concatenate(
                    [jnp.broadcast_to(v[z : z + 1, :], (8, 128)) * mask for v in values], axis=0
                )
                high = tall.astype(BF16)
                low = (tall - high.astype(F32)).astype(BF16)
                spread[:, pl.ds(128 * c, 128)] = jnp.concatenate([high, low], axis=0)
        sent = lax.dot_general(
            spread[...], onehot[...], (((1,), (1,)), ((), ())), preferred_element_type=F32
        )
        sent = sent[0:24] + sent[24:48]
        numer = [numer[a] + sent[8 * a : 8 * a + 8] for a in range(2)]
        denom = denom + sent[16:24]
        if n > 0:
            for side in (0, 1):
                halo_copy(n - 1, side).wait_recv()
            base = 32 * (n - 1)
            below = [jnp.where(y > 0, halo[pl.ds(base + 8 * a, 8), :], 0.0) for a in range(2)]
            above = [jnp.where(y < ny - 1, halo[pl.ds(base + 16 + 8 * a, 8), :], 0.0) for a in range(2)]
            numer = [LAMBDA * (below[a] + above[a]) + numer[a] for a in range(2)]
        field = [numer[a] / (2.0 * LAMBDA + denom) for a in range(2)]
        if n < 2:
            for a in range(2):
                fsend[pl.ds(16 * n + 8 * a, 8), :] = field[a]
            for side in (0, 1):
                halo_copy(n, side).start()

    for a in range(2):
        mine = jnp.sum(jnp.where(down8 == mz, field[a], 0.0), axis=0, keepdims=True)
        turned = pltpu.roll(jnp.broadcast_to(mine, (8, 128)), lax.rem(128 - DATE_DEV * me, 128), 1)
        disp_out[a] = turned[0:1, :DATE_DEV]

    for k in range(1, ROW):
        row_copy(k).wait_send()
        mrow_copy(k).wait_send()
    for k in range(1, NZ):
        zsec_copy(k).wait_send()
        mall_copy(k).wait_send()
    for s in (1, 2, 3):
        for half in (0, 1):
            plus_copy(s, half).wait_send()
            minus_copy(s, half).wait_send()
    plus_copy(4, 0).wait_send()
    minus_copy(4, 1).wait_send()
    for t in range(NZ):
        for k in range(1, ROW):
            x_copy(t, k, block_of(t)).wait_send()
    for n in range(2):
        for side in (0, 1):
            halo_copy(n, side).wait_send()


def per_device(chips, pair_target, pair_slot, offset_fix):
    flat = chips.reshape(DATE_DEV, CHIP * CHIP)
    target = pair_target.reshape(1, PAIRS)
    slot = pair_slot.reshape(1, PAIRS)
    offs = jnp.transpose(offset_fix.reshape(PAIRS, 2), (1, 0))
    vmem = pl.BlockSpec(memory_space=pltpu.VMEM)
    smem = pl.BlockSpec(memory_space=pltpu.SMEM)
    dma = pltpu.SemaphoreType.DMA
    measure, disp = pl.pallas_call(
        kernel,
        out_shape=(
            jax.ShapeDtypeStruct((3, 1, PAIRS), F32),
            jax.ShapeDtypeStruct((2, 1, DATE_DEV), F32),
        ),
        in_specs=[vmem, vmem, vmem, smem, vmem],
        out_specs=(vmem, vmem),
        scratch_shapes=[
            pltpu.VMEM((DATE_DEV * 32 + 32, 128), F32),
            *[pltpu.VMEM((DATE_DEV, 32, 128), BF16)] * NZ,
            pltpu.VMEM((NZ * ROW * 2, 32, 128), BF16),
            pltpu.VMEM((NZ * ROW * 2, 32, 128), BF16),
            pltpu.VMEM((DATE_DEV * 8, 128), F32),
            pltpu.VMEM((ROW * 16 + 8, 128), F32),
            pltpu.VMEM((NZ * 8 + 8, 128), F32),
            pltpu.VMEM((16, 128), jnp.int32),
            pltpu.SMEM((16, 128), jnp.int32),
            pltpu.VMEM((PAIRS, 32, 384), BF16),
            pltpu.VMEM((PAIRS, 96, 128), BF16),
            pltpu.VMEM((128, LINKS * NZ * 128), BF16),
            pltpu.VMEM((LINKS * NZ * 8, 128), F32),
            pltpu.VMEM((9 * ITEMS * PAIRS, 128), F32),
            pltpu.VMEM((ROW * 16, 128), F32),
            pltpu.VMEM((NZ * 16 + 16, 128), F32),
            pltpu.VMEM((48, LINKS * NZ * 128), BF16),
            pltpu.VMEM((32, 128), F32),
            pltpu.VMEM((64, 128), F32),
            dma,
            dma((ROW,)),
            dma((ROW,)),
            dma((NZ,)),
            dma((NZ,)),
            dma((4, 2)),
            dma((4, 2)),
            dma((4, 2)),
            dma((4, 2)),
            dma((NZ, ROW)),
            dma((NZ, ROW)),
            dma((ROW,)),
            dma((ROW,)),
            dma((NZ,)),
            dma((NZ,)),
            dma((2, 2)),
            dma((2, 2)),
        ],
        compiler_params=pltpu.CompilerParams(
            collective_id=0, has_side_effects=True, vmem_limit_bytes=40 * 1024 * 1024
        ),
        name="offset_network",
    )(flat, target, slot, offs, offs)
    return (jnp.transpose(disp, (0, 2, 1)), jnp.transpose(measure, (0, 2, 1)))


def solution(mesh):
    in_specs = (P("date", "space", None), P("date", None), P("date"), P("date", "space", None))
    out_specs = (P(None, "date", "space"), P(None, "date", "space"))
    return jax.shard_map(
        per_device, mesh=mesh, in_specs=in_specs, out_specs=out_specs, check_vma=False
    )
```

```python
import jax
import jax.numpy as jnp
from jax import lax
from jax.experimental import pallas as pl
from jax.experimental.pallas import tpu as pltpu
from jax.sharding import PartitionSpec as P

CHIP = 64
LINKS = 4
ROW = 8
NZ = 8
DATE_DEV = 16
PAIRS = 64
CHUNKS = 4
CHUNK = DATE_DEV // CHUNKS
SIGMA = 0.6
ZSCALE = 0.5
EPS = 1e-06
LAMBDA = 2.0
MUS = (4.0, 2.0, 1.0)
FIXED = 32.0
ITEMS = 11
F32 = jnp.float32
BF16 = jnp.bfloat16
PRE = (6, 4, 3, 3)


def iota(shape, dim):
    return lax.broadcasted_iota(jnp.int32, shape, dim)


def fold(rows):
    return jnp.sum(rows.reshape(rows.shape[0] // 8, 8, 128), axis=0)


def split_bf16(value):
    high = value.astype(BF16)
    return high, (value - high.astype(F32)).astype(BF16)


def kernel(
    chips_in,
    target_in,
    slot_in,
    offs_in,
    measure_out,
    disp_out,
    chips,
    target,
    slot,
    offs_s,
    offs_v,
    tmp,
    held0,
    held1,
    held2,
    held3,
    held4,
    held5,
    held6,
    held7,
    xsend,
    recv,
    bnorm,
    rowx,
    zsec,
    reqv,
    req,
    mbuf,
    lhs,
    onehot,
    member,
    sums,
    mrow,
    mall,
    spread,
    fsend,
    halo,
    sem_in,
    sem_req,
    row_s,
    row_r,
    zsec_s,
    zsec_r,
    plus_s,
    plus_r,
    minus_s,
    minus_r,
    x_s,
    x_r,
    mrow_s,
    mrow_r,
    mall_s,
    mall_r,
    halo_s,
    halo_r,
):
    held = (held0, held1, held2, held3, held4, held5, held6, held7)
    date = lax.axis_index("date")
    y = lax.axis_index("space")
    ny = lax.axis_size("space")
    mz = lax.div(date, ROW)
    me = lax.rem(date, ROW)

    def row_peer(k):
        return {"date": mz * ROW + lax.rem(me + k, ROW)}

    def z_peer(k):
        return {"date": lax.rem(mz + k, NZ) * ROW + me}

    def y_peer(k):
        return {"space": lax.rem(y + k, ny)}

    def remote(src, dst, ssem, rsem, peer):
        return pltpu.make_async_remote_copy(
            src_ref=src,
            dst_ref=dst,
            send_sem=ssem,
            recv_sem=rsem,
            device_id=peer,
            device_id_type=pl.DeviceIdType.MESH,
        )

    barrier = pltpu.get_barrier_semaphore()
    for k in range(1, ROW):
        pl.semaphore_signal(barrier, inc=1, device_id=row_peer(k), device_id_type=pl.DeviceIdType.MESH)
    for k in range(1, NZ):
        pl.semaphore_signal(barrier, inc=1, device_id=z_peer(k), device_id_type=pl.DeviceIdType.MESH)
    for k in (1, 2, ny - 2, ny - 1):
        pl.semaphore_signal(barrier, inc=1, device_id=y_peer(k), device_id_type=pl.DeviceIdType.MESH)

    loads = [
        pltpu.make_async_copy(src, dst, sem_in.at[n])
        for n, (src, dst) in enumerate(
            ((target_in, target), (slot_in, slot), (chips_in, chips), (offs_in, offs_s), (offs_in, offs_v))
        )
    ]
    for load in loads:
        load.start()
    for load in loads:
        load.wait()

    for j in range(32):
        tmp[pl.ds(j, DATE_DEV, stride=32), :] = chips[:, 128 * j : 128 * j + 128].astype(F32)
    for d in range(DATE_DEV):
        own = tmp[pl.ds(32 * d, 32), :]
        held[0][d] = own.astype(BF16)
        bnorm[pl.ds(8 * d, 8), :] = fold(own * own)

    sub = iota((PAIRS, 128), 0)
    lane = iota((PAIRS, 128), 1)
    zeros64 = jnp.zeros((1, 128 - PAIRS), jnp.int32)
    trow = jnp.concatenate([target[...], zeros64 - 1], axis=1).astype(F32)
    srow = jnp.concatenate([slot[...], zeros64], axis=1).astype(F32)
    tb = jnp.broadcast_to(trow, (PAIRS, 128))
    sb = jnp.broadcast_to(srow, (PAIRS, 128))
    eye = sub == lane
    tcol = jnp.sum(jnp.where(eye, tb, 0.0), axis=1, keepdims=True)
    scol = jnp.sum(jnp.where(eye, sb, 0.0), axis=1, keepdims=True)
    twin = jnp.where((tcol == tb) & (lane < sub), 1.0, 0.0)
    place = 2.0 * tcol + jnp.sum(twin, axis=1, keepdims=True)
    wanted = jnp.sum(jnp.where(lane.astype(F32) == place, scol, 0.0), axis=0, keepdims=True)
    place_row = jnp.sum(jnp.where(eye, place, 0.0), axis=0, keepdims=True)
    deal = jnp.where(lane == me * DATE_DEV + sub // LINKS, 1.0, 0.0).astype(BF16)
    r8 = iota((8, PAIRS), 0)
    l8 = iota((8, PAIRS), 1)
    ours = (l8 % LINKS) == (r8 % LINKS)
    named = jnp.where(r8 < 4, jnp.broadcast_to(trow[:, :PAIRS], (8, PAIRS)), jnp.broadcast_to(srow[:, :PAIRS], (8, PAIRS)))
    named = jnp.where(ours, named, 0.0).astype(BF16)
    rowx[pl.ds(0, 8), :] = jnp.dot(named, deal, preferred_element_type=F32)
    rowx[pl.ds(8, 8), :] = jnp.broadcast_to(wanted, (8, 128))

    pl.semaphore_wait(barrier, ROW - 1 + NZ - 1 + 4)

    def row_copy(k):
        return remote(rowx.at[pl.ds(0, 16)], rowx.at[pl.ds(16 * k, 16)], row_s.at[k], row_r.at[k], row_peer(k))

    def ring_part(t, c):
        return held[t].at[pl.ds(c * CHUNK, CHUNK)]

    def plus_copy(s, c):
        return remote(
            ring_part(max(2 * s - 3, 0), c),
            ring_part(2 * s - 1, c),
            plus_s.at[s - 1, c],
            plus_r.at[s - 1, c],
            z_peer(1),
        )

    def minus_copy(s, c):
        return remote(
            ring_part(2 * s - 2, c),
            ring_part(min(2 * s, 7), c),
            minus_s.at[s - 1, c],
            minus_r.at[s - 1, c],
            z_peer(NZ - 1),
        )

    def goes_plus(s, c):
        return s < 4 or c < CHUNKS // 2

    def goes_minus(s, c):
        return s < 4 or c >= CHUNKS // 2

    for k in range(1, ROW):
        row_copy(k).start()
    for c in range(CHUNKS):
        plus_copy(1, c).start()
        minus_copy(1, c).start()

    lane64 = iota((CHIP, 128), 1)
    spacing_x = ((lane64 % CHIP) - iota((CHIP, 128), 0)).astype(F32)
    left64 = lane64 < CHIP
    lane32 = iota((32, 128), 1)
    q32 = lane32 % CHIP
    m32 = 2 * (q32 % 32) + q32 // 32
    spacing_y = (m32 - 2 * iota((32, 128), 0) - lane32 // CHIP).astype(F32)
    left32 = lane32 < CHIP
    decay = -1.0 / (2.0 * SIGMA * SIGMA)

    def prepare(d, carry):
        own = held[0][d]
        for l in range(LINKS):
            i = d * LINKS + l
            off_y = offs_s[0, i].astype(F32) * (1.0 / FIXED)
            off_x = offs_s[1, i].astype(F32) * (1.0 / FIXED)
            tops, bottoms = [], []
            for level in (-1.0, 0.0, 1.0):
                gap = spacing_x - (off_x + level)
                bell = jnp.exp(gap * gap * decay)
                tops.append(jnp.where(left64, bell, 0.0).astype(BF16))
                bottoms.append(jnp.where(left64, 0.0, bell).astype(BF16))
            wide = jnp.concatenate([jnp.concatenate(tops, axis=1), jnp.concatenate(bottoms, axis=1)], axis=0)
            mbuf[i] = jnp.dot(own, wide, preferred_element_type=F32).astype(BF16)
            for e, level in enumerate((-1.0, 0.0, 1.0)):
                gap = spacing_y - (off_y + level)
                lhs[i, pl.ds(32 * e, 32), :] = jnp.exp(gap * gap * decay).astype(BF16)
        return carry

    def prepare_part(n):
        low = sum(PRE[:n])
        lax.fori_loop(low, low + PRE[n], prepare, 0)

    prepare_part(0)
    for k in range(1, ROW):
        row_copy(k).wait_recv()

    reqv[pl.ds(0, 8), :] = rowx[pl.ds(8, 8, stride=16), :].astype(jnp.int32)
    reqv[pl.ds(8, 8), :] = jnp.broadcast_to(place_row, (8, 128)).astype(jnp.int32)
    fetch = pltpu.make_async_copy(reqv, req, sem_req)
    fetch.start()
    total = rowx[pl.ds(0, 8), :]
    for k in range(1, ROW):
        total = total + rowx[pl.ds(16 * k, 8), :]
    zsec[pl.ds(8 * mz, 8), :] = total

    def zsec_copy(k):
        mine = zsec.at[pl.ds(8 * mz, 8)]
        return remote(mine, mine, zsec_s.at[k], zsec_r.at[k], z_peer(k))

    def zsec_arrived(k):
        theirs = zsec.at[pl.ds(8 * lax.rem(mz - k + NZ, NZ), 8)]
        remote(theirs, theirs, zsec_s.at[k], zsec_r.at[k], z_peer(k)).wait_recv()

    fetch.wait()

    def x_copy(t, k, block):
        return remote(
            xsend.at[pl.ds((t * ROW + k) * 2, 2)],
            recv.at[pl.ds(block * 16 + me * 2, 2)],
            x_s.at[t, k],
            x_r.at[t, k],
            row_peer(k),
        )

    def x_arrived(t, k, block):
        theirs = recv.at[pl.ds(block * 16 + lax.rem(me - k + ROW, ROW) * 2, 2)]
        remote(xsend.at[pl.ds((t * ROW + k) * 2, 2)], theirs, x_s.at[t, k], x_r.at[t, k], row_peer(k)).wait_recv()

    def block_of(t):
        step = (t + 1) // 2
        return lax.rem(mz - step + NZ, NZ) if t % 2 else lax.rem(mz + step, NZ)

    def serve(t):
        block = block_of(t)
        for k in (1, 7, 2, 6, 3, 5, 4, 0):
            asker = (ROW - k) % ROW
            for r in (0, 1):
                chip = held[t][jnp.clip(req[asker, block * 16 + me * 2 + r], 0, DATE_DEV - 1)]
                if k:
                    xsend[(t * ROW + k) * 2 + r] = chip
                else:
                    recv[block * 16 + me * 2 + r] = chip
            if k:
                x_copy(t, k, block).start()

    serve(0)
    for k in range(1, NZ):
        zsec_copy(k).start()
    for s in (1, 2, 3):
        for c in range(CHUNKS):
            plus_copy(s, c).wait_recv()
            if goes_plus(s + 1, c):
                plus_copy(s + 1, c).start()
            minus_copy(s, c).wait_recv()
            if goes_minus(s + 1, c):
                minus_copy(s + 1, c).start()
        serve(2 * s - 1)
        serve(2 * s)
        prepare_part(s)
    for k in range(1, NZ):
        zsec_arrived(k)

    later = []
    for l in range(LINKS):
        dev = zsec[pl.ds(l, NZ, stride=8), :].astype(jnp.int32)
        pos = zsec[pl.ds(4 + l, NZ, stride=8), :].astype(jnp.int32)
        later.append((dev // ROW, (dev % ROW) * DATE_DEV + pos))
    down128 = iota((128, 128), 0)
    down8 = iota((8, 128), 0)
    for l in range(LINKS):
        for z in range(NZ):
            c = l * NZ + z
            hit = jnp.broadcast_to(later[l][1][z : z + 1, :], (128, 128)) == down128
            onehot[:, pl.ds(128 * c, 128)] = jnp.where(hit, 1.0, 0.0).astype(BF16)
            hit = jnp.broadcast_to(later[l][0][z : z + 1, :], (8, 128)) == down8
            member[pl.ds(8 * c, 8), :] = jnp.where(hit, 1.0, 0.0)

    for c in range(CHUNKS):
        (plus_copy if goes_plus(4, c) else minus_copy)(4, c).wait_recv()
    serve(7)
    for t in range(NZ):
        for k in range(1, ROW):
            x_arrived(t, k, block_of(t))

    def score(d, carry):
        pairs = [d * LINKS + l for l in range(LINKS)]
        chip = [recv[jnp.clip(req[8, i], 0, NZ * ROW * 2 - 1)].astype(F32) for i in pairs]
        lifted = []
        for l, i in enumerate(pairs):
            swapped = pltpu.roll(chip[l], CHIP, 1)
            blocks = jnp.concatenate(
                [
                    jnp.where(left32, chip[l], 0.0).astype(BF16),
                    jnp.where(left32, swapped, 0.0).astype(BF16),
                    jnp.where(left32, 0.0, swapped).astype(BF16),
                    jnp.where(left32, 0.0, chip[l]).astype(BF16),
                ],
                axis=0,
            )
            lifted.append(jnp.dot(lhs[i], blocks, preferred_element_type=F32).astype(BF16))
        for l, i in enumerate(pairs):
            up = lifted[l].astype(F32)
            moved = mbuf[i].astype(F32)
            for ky in range(3):
                for kx in range(3):
                    part = fold(up[32 * ky : 32 * ky + 32] * moved[:, 128 * kx : 128 * kx + 128])
                    sums[pl.ds((3 * ky + kx) * PAIRS + i, 8, stride=ITEMS * PAIRS), :] = part
            sums[pl.ds(9 * PAIRS + i, 8, stride=ITEMS * PAIRS), :] = fold(chip[l] * chip[l])
            sums[pl.ds(10 * PAIRS + i, 8, stride=ITEMS * PAIRS), :] = bnorm[pl.ds(8 * d, 8), :]
        return carry

    lax.fori_loop(0, DATE_DEV, score, 0)

    rows = []
    for item in range(ITEMS):
        part = sums[pl.ds(item * PAIRS, PAIRS), :]
        for s in range(1, 8):
            part = part + sums[pl.ds(s * ITEMS * PAIRS + item * PAIRS, PAIRS), :]
        rows.append(jnp.sum(part.T, axis=0, keepdims=True))
    size = CHIP / jnp.sqrt((rows[10] + EPS) * (rows[9] + EPS))
    scores = [rows[q] * size for q in range(9)]
    raised = [jnp.exp(ZSCALE * s) for s in scores]
    whole = raised[0]
    for q in range(1, 9):
        whole = whole + raised[q]
    weights = [r / whole for r in raised]
    offs = offs_v[...].astype(F32) * (1.0 / FIXED)
    move_y = offs[0:1] + ((weights[6] + weights[7] + weights[8]) - (weights[0] + weights[1] + weights[2]))
    move_x = offs[1:2] + ((weights[2] + weights[5] + weights[8]) - (weights[0] + weights[3] + weights[6]))
    blend = weights[0] * scores[0]
    for q in range(1, 9):
        blend = blend + weights[q] * scores[q]
    quality = 1.0 / (1.0 + jnp.exp(-ZSCALE * blend))
    measure_out[0] = move_y
    measure_out[1] = move_x
    measure_out[2] = quality

    up = jnp.where(r8 < 4, jnp.broadcast_to(move_y, (8, PAIRS)), jnp.broadcast_to(move_x, (8, PAIRS)))
    up = jnp.where(ours, up, 0.0)
    down = jnp.where(ours & (r8 < 4), jnp.broadcast_to(quality, (8, PAIRS)), 0.0)
    both = jnp.concatenate([up, down], axis=0)
    first = both.astype(BF16)
    rest = both - first.astype(F32)
    second = rest.astype(BF16)
    third = (rest - second.astype(F32)).astype(BF16)
    dealt = jnp.dot(jnp.concatenate([first, second, third], axis=0), deal, preferred_element_type=F32)
    mrow[pl.ds(0, 16), :] = dealt[0:16] + dealt[16:32] + dealt[32:48]

    def mrow_copy(k):
        return remote(mrow.at[pl.ds(0, 16)], mrow.at[pl.ds(16 * k, 16)], mrow_s.at[k], mrow_r.at[k], row_peer(k))

    for k in range(1, ROW):
        mrow_copy(k).start()
    for k in range(1, ROW):
        mrow_copy(k).wait_recv()
    total = mrow[pl.ds(0, 16), :]
    for k in range(1, ROW):
        total = total + mrow[pl.ds(16 * k, 16), :]
    mall[pl.ds(16 * mz, 16), :] = total

    def mall_copy(k):
        mine = mall.at[pl.ds(16 * mz, 16)]
        return remote(mine, mine, mall_s.at[k], mall_r.at[k], z_peer(k))

    def mall_arrived(k):
        theirs = mall.at[pl.ds(16 * lax.rem(mz - k + NZ, NZ), 16)]
        remote(theirs, theirs, mall_s.at[k], mall_r.at[k], z_peer(k)).wait_recv()

    for k in range(1, NZ):
        mall_copy(k).start()
    for k in range(1, NZ):
        mall_arrived(k)

    meas = [[mall[pl.ds(4 * a + l, NZ, stride=16), :] for l in range(LINKS)] for a in range(2)]
    qual = [mall[pl.ds(8 + l, NZ, stride=16), :] for l in range(LINKS)]
    field = None

    def halo_copy(n, side):
        peer = y_peer((1, ny - 1, 2, ny - 2)[side])
        if n == 0:
            return remote(fsend.at[pl.ds(0, 16)], halo.at[side, pl.ds(0, 16)], halo_s.at[0, side], halo_r.at[0, side], peer)
        return remote(fsend.at[pl.ds(16, 24)], halo.at[side, pl.ds(16, 24)], halo_s.at[1, side], halo_r.at[1, side], peer)

    def inside(steps, value):
        return jnp.where((y + steps >= 0) & (y + steps < ny), value, 0.0)

    def settle(beside, numer, denom):
        return [(LAMBDA * beside[a] + numer[a]) / (2.0 * LAMBDA + denom) for a in range(2)]

    for n, scale in enumerate(MUS):
        square = scale * scale
        numer = [None, None]
        denom = None
        for l in range(LINKS):
            if field is None:
                here = [0.0, 0.0]
                there = [0.0, 0.0]
            else:
                here = field
                there = []
                for a in range(2):
                    got = None
                    for z in range(NZ):
                        table = jnp.broadcast_to(field[a][z : z + 1, :], (NZ, 128))
                        found = jnp.take_along_axis(table, later[l][1], axis=1, mode="promise_in_bounds")
                        got = found if got is None else jnp.where(later[l][0] == z, found, got)
                    there.append(got)
            resid = [meas[a][l] - (there[a] - here[a]) for a in range(2)]
            gnc = qual[l] * square / (square + (resid[0] * resid[0] + resid[1] * resid[1]))
            values = [gnc * (here[a] + meas[a][l]) for a in range(2)] + [gnc]
            for a in range(2):
                back = gnc * (there[a] - meas[a][l])
                numer[a] = back if l == 0 else numer[a] + back
            denom = gnc if l == 0 else denom + gnc
            for z in range(NZ):
                c = l * NZ + z
                mask = member[pl.ds(8 * c, 8), :]
                tall = jnp.concatenate(
                    [jnp.broadcast_to(v[z : z + 1, :], (8, 128)) * mask for v in values], axis=0
                )
                high = tall.astype(BF16)
                low = (tall - high.astype(F32)).astype(BF16)
                spread[:, pl.ds(128 * c, 128)] = jnp.concatenate([high, low], axis=0)
        sent = lax.dot_general(
            spread[...], onehot[...], (((1,), (1,)), ((), ())), preferred_element_type=F32
        )
        sent = sent[0:24] + sent[24:48]
        numer = [numer[a] + sent[8 * a : 8 * a + 8] for a in range(2)]
        denom = denom + sent[16:24]
        if n == 0:
            field = [numer[a] / (2.0 * LAMBDA + denom) for a in range(2)]
            for a in range(2):
                fsend[pl.ds(8 * a, 8), :] = field[a]
            for side in range(4):
                halo_copy(0, side).start()
        elif n == 1:
            for a in range(2):
                fsend[pl.ds(16 + 8 * a, 8), :] = numer[a]
            fsend[pl.ds(32, 8), :] = denom
            for side in (0, 1):
                halo_copy(1, side).start()
            for side in range(4):
                halo_copy(0, side).wait_recv()
            near = [inside(-1, halo[0, pl.ds(8 * a, 8), :]) + inside(1, halo[1, pl.ds(8 * a, 8), :]) for a in range(2)]
            start = field
            field = settle(near, numer, denom)
        else:
            for side in (0, 1):
                halo_copy(1, side).wait_recv()
            beside = [0.0, 0.0]
            for side, way in ((0, -1), (1, 1)):
                reach = [start[a] + inside(2 * way, halo[2 + side, pl.ds(8 * a, 8), :]) for a in range(2)]
                theirs = [halo[side, pl.ds(16 + 8 * a, 8), :] for a in range(2)]
                there = settle(reach, theirs, halo[side, pl.ds(32, 8), :])
                beside = [beside[a] + inside(way, there[a]) for a in range(2)]
            field = settle(beside, numer, denom)

    for a in range(2):
        mine = jnp.sum(jnp.where(down8 == mz, field[a], 0.0), axis=0, keepdims=True)
        turned = pltpu.roll(jnp.broadcast_to(mine, (8, 128)), lax.rem(128 - DATE_DEV * me, 128), 1)
        disp_out[a] = turned[0:1, :DATE_DEV]

    for k in range(1, ROW):
        row_copy(k).wait_send()
        mrow_copy(k).wait_send()
    for k in range(1, NZ):
        zsec_copy(k).wait_send()
        mall_copy(k).wait_send()
    for s in (1, 2, 3, 4):
        for c in range(CHUNKS):
            if goes_plus(s, c):
                plus_copy(s, c).wait_send()
            if goes_minus(s, c):
                minus_copy(s, c).wait_send()
    for t in range(NZ):
        for k in range(1, ROW):
            x_copy(t, k, block_of(t)).wait_send()
    for n, side in ((0, 0), (0, 1), (0, 2), (0, 3), (1, 0), (1, 1)):
        halo_copy(n, side).wait_send()


def per_device(chips, pair_target, pair_slot, offset_fix):
    flat = chips.reshape(DATE_DEV, CHIP * CHIP)
    target = pair_target.reshape(1, PAIRS)
    slot = pair_slot.reshape(1, PAIRS)
    offs = jnp.transpose(offset_fix.reshape(PAIRS, 2), (1, 0))
    vmem = pl.BlockSpec(memory_space=pltpu.VMEM)
    anywhere = pl.BlockSpec(memory_space=pl.ANY)
    dma = pltpu.SemaphoreType.DMA
    measure, disp = pl.pallas_call(
        kernel,
        out_shape=(
            jax.ShapeDtypeStruct((3, 1, PAIRS), F32),
            jax.ShapeDtypeStruct((2, 1, DATE_DEV), F32),
        ),
        in_specs=[anywhere] * 4,
        out_specs=(vmem, vmem),
        scratch_shapes=[
            pltpu.VMEM((DATE_DEV, CHIP * CHIP), BF16),
            pltpu.VMEM((1, PAIRS), jnp.int32),
            pltpu.VMEM((1, PAIRS), jnp.int32),
            pltpu.SMEM((2, PAIRS), jnp.int32),
            pltpu.VMEM((2, PAIRS), jnp.int32),
            pltpu.VMEM((DATE_DEV * 32 + 32, 128), F32),
            *[pltpu.VMEM((DATE_DEV, 32, 128), BF16)] * NZ,
            pltpu.VMEM((NZ * ROW * 2, 32, 128), BF16),
            pltpu.VMEM((NZ * ROW * 2, 32, 128), BF16),
            pltpu.VMEM((DATE_DEV * 8, 128), F32),
            pltpu.VMEM((ROW * 16 + 8, 128), F32),
            pltpu.VMEM((NZ * 8 + 8, 128), F32),
            pltpu.VMEM((16, 128), jnp.int32),
            pltpu.SMEM((16, 128), jnp.int32),
            pltpu.VMEM((PAIRS, 32, 384), BF16),
            pltpu.VMEM((PAIRS, 96, 128), BF16),
            pltpu.VMEM((128, LINKS * NZ * 128), BF16),
            pltpu.VMEM((LINKS * NZ * 8, 128), F32),
            pltpu.VMEM((9 * ITEMS * PAIRS, 128), F32),
            pltpu.VMEM((ROW * 16, 128), F32),
            pltpu.VMEM((NZ * 16 + 16, 128), F32),
            pltpu.VMEM((48, LINKS * NZ * 128), BF16),
            pltpu.VMEM((40, 128), F32),
            pltpu.VMEM((4, 40, 128), F32),
            dma((5,)),
            dma,
            dma((ROW,)),
            dma((ROW,)),
            dma((NZ,)),
            dma((NZ,)),
            dma((4, CHUNKS)),
            dma((4, CHUNKS)),
            dma((4, CHUNKS)),
            dma((4, CHUNKS)),
            dma((NZ, ROW)),
            dma((NZ, ROW)),
            dma((ROW,)),
            dma((ROW,)),
            dma((NZ,)),
            dma((NZ,)),
            dma((2, 4)),
            dma((2, 4)),
        ],
        compiler_params=pltpu.CompilerParams(
            collective_id=0, has_side_effects=True, vmem_limit_bytes=40 * 1024 * 1024
        ),
        name="offset_network",
    )(flat, target, slot, offs)
    return (jnp.transpose(disp, (0, 2, 1)), jnp.transpose(measure, (0, 2, 1)))


def solution(mesh):
    in_specs = (P("date", "space", None), P("date", None), P("date"), P("date", "space", None))
    out_specs = (P(None, "date", "space"), P(None, "date", "space"))
    return jax.shard_map(
        per_device, mesh=mesh, in_specs=in_specs, out_specs=out_specs, check_vma=False
    )
```

```python
import jax
import jax.numpy as jnp
from jax import lax
from jax.experimental import pallas as pl
from jax.experimental.pallas import tpu as pltpu
from jax.sharding import PartitionSpec as P

CHIP = 64
LINKS = 4
ROW = 8
NZ = 8
DATE_DEV = 16
PAIRS = 64
CHUNKS = 4
CHUNK = DATE_DEV // CHUNKS
SIGMA = 0.6
ZSCALE = 0.5
EPS = 1e-06
LAMBDA = 2.0
MUS = (4.0, 2.0, 1.0)
FIXED = 32.0
ITEMS = 11
F32 = jnp.float32
BF16 = jnp.bfloat16
PRE = (7, 1, 2, 2, 4)
SLOTS = 128
GROUPS = ((0,), (1, 2), (3, 4), (5, 6), (7,))


def iota(shape, dim):
    return lax.broadcasted_iota(jnp.int32, shape, dim)


def fold(rows):
    return jnp.sum(rows.reshape(rows.shape[0] // 8, 8, 128), axis=0)


def thirds_dot(value, chosen):
    first = value.astype(BF16)
    rest = value - first.astype(F32)
    second = rest.astype(BF16)
    third = (rest - second.astype(F32)).astype(BF16)
    out = jnp.dot(jnp.concatenate([first, second, third], axis=0), chosen, preferred_element_type=F32)
    n = value.shape[0]
    return out[:n] + out[n : 2 * n] + out[2 * n :]


def kernel(
    chips_in,
    target_in,
    slot_in,
    offs_in,
    measure_out,
    disp_out,
    chips,
    target,
    slot,
    offs_s,
    offs_v,
    tmp,
    held0,
    held1,
    held2,
    held3,
    held4,
    held5,
    held6,
    held7,
    xsend,
    recv,
    bnorm,
    rowx,
    zsec,
    reqv,
    req,
    mbuf,
    lhs,
    onehot,
    member,
    sums,
    mrow,
    mall,
    spread,
    fsend,
    halo,
    sem_in,
    sem_req,
    row_s,
    row_r,
    zsec_s,
    zsec_r,
    plus_s,
    plus_r,
    minus_s,
    minus_r,
    x_s,
    x_r,
    mrow_s,
    mrow_r,
    mall_s,
    mall_r,
    halo_s,
    halo_r,
):
    held = (held0, held1, held2, held3, held4, held5, held6, held7)
    date = lax.axis_index("date")
    y = lax.axis_index("space")
    ny = lax.axis_size("space")
    mz = lax.div(date, ROW)
    me = lax.rem(date, ROW)

    def row_peer(k):
        return {"date": mz * ROW + lax.rem(me + k, ROW)}

    def z_peer(k):
        return {"date": lax.rem(mz + k, NZ) * ROW + me}

    def y_peer(k):
        return {"space": lax.rem(y + k, ny)}

    def remote(src, dst, ssem, rsem, peer):
        return pltpu.make_async_remote_copy(
            src_ref=src,
            dst_ref=dst,
            send_sem=ssem,
            recv_sem=rsem,
            device_id=peer,
            device_id_type=pl.DeviceIdType.MESH,
        )

    barrier = pltpu.get_barrier_semaphore()
    for k in range(1, ROW):
        pl.semaphore_signal(barrier, inc=1, device_id=row_peer(k), device_id_type=pl.DeviceIdType.MESH)
    for k in range(1, NZ):
        pl.semaphore_signal(barrier, inc=1, device_id=z_peer(k), device_id_type=pl.DeviceIdType.MESH)
    for k in (1, 2, ny - 2, ny - 1):
        pl.semaphore_signal(barrier, inc=1, device_id=y_peer(k), device_id_type=pl.DeviceIdType.MESH)

    loads = [
        pltpu.make_async_copy(src, dst, sem_in.at[n])
        for n, (src, dst) in enumerate(
            ((chips_in, chips), (target_in, target), (slot_in, slot), (offs_in, offs_s), (offs_in, offs_v))
        )
    ]
    for load in loads:
        load.start()
    for load in loads[1:]:
        load.wait()

    sub = iota((PAIRS, 128), 0)
    lane = iota((PAIRS, 128), 1)
    zeros64 = jnp.zeros((1, 128 - PAIRS), jnp.int32)
    trow = jnp.concatenate([target[...], zeros64 - 1], axis=1).astype(F32)
    srow = jnp.concatenate([slot[...], zeros64], axis=1).astype(F32)
    tb = jnp.broadcast_to(trow, (PAIRS, 128))
    sb = jnp.broadcast_to(srow, (PAIRS, 128))
    eye = sub == lane
    tcol = jnp.sum(jnp.where(eye, tb, 0.0), axis=1, keepdims=True)
    scol = jnp.sum(jnp.where(eye, sb, 0.0), axis=1, keepdims=True)
    twin = jnp.where((tcol == tb) & (lane < sub), 1.0, 0.0)
    rank = jnp.sum(twin, axis=1, keepdims=True).astype(jnp.int32)
    holder = tcol.astype(jnp.int32)
    away = (holder // ROW - mz + NZ) % NZ
    turn = jnp.where(away < NZ // 2, 2 * away, 2 * NZ - 1 - 2 * away)
    place = turn * (2 * ROW) + (holder % ROW) * 2 + rank
    wanted = jnp.sum(jnp.where(lane == place, scol, 0.0), axis=0, keepdims=True)
    pair_of = jnp.sum(jnp.where(lane == place, sub.astype(F32), 0.0), axis=0, keepdims=True)
    place_row = jnp.sum(jnp.where(eye, place.astype(F32), 0.0), axis=0, keepdims=True)
    deal = jnp.where(lane == me * DATE_DEV + sub // LINKS, 1.0, 0.0).astype(BF16)
    r8 = iota((8, PAIRS), 0)
    l8 = iota((8, PAIRS), 1)
    ours = (l8 % LINKS) == (r8 % LINKS)
    named = jnp.where(r8 < 4, jnp.broadcast_to(trow[:, :PAIRS], (8, PAIRS)), jnp.broadcast_to(srow[:, :PAIRS], (8, PAIRS)))
    named = jnp.where(ours, named, 0.0).astype(BF16)
    rowx[pl.ds(0, 8), :] = jnp.dot(named, deal, preferred_element_type=F32)
    rowx[pl.ds(8, 8), :] = jnp.broadcast_to(wanted, (8, 128))

    loads[0].wait()
    for j in range(32):
        tmp[pl.ds(j, DATE_DEV, stride=32), :] = chips[:, 128 * j : 128 * j + 128].astype(F32)
    for d in range(DATE_DEV):
        own = tmp[pl.ds(32 * d, 32), :]
        held[0][d] = own.astype(BF16)
        bnorm[d] = fold(own * own)

    pl.semaphore_wait(barrier, ROW - 1 + NZ - 1 + 4)

    def row_copy(k):
        return remote(rowx.at[pl.ds(0, 16)], rowx.at[pl.ds(16 * k, 16)], row_s.at[k], row_r.at[k], row_peer(k))

    def ring_part(t, c):
        return held[t].at[pl.ds(c * CHUNK, CHUNK)]

    def plus_copy(s, c):
        return remote(
            ring_part(max(2 * s - 3, 0), c),
            ring_part(2 * s - 1, c),
            plus_s.at[s - 1, c],
            plus_r.at[s - 1, c],
            z_peer(1),
        )

    def minus_copy(s, c):
        return remote(
            ring_part(2 * s - 2, c),
            ring_part(min(2 * s, 7), c),
            minus_s.at[s - 1, c],
            minus_r.at[s - 1, c],
            z_peer(NZ - 1),
        )

    def goes_plus(s, c):
        return s < 4 or c < CHUNKS // 2

    def goes_minus(s, c):
        return s < 4 or c >= CHUNKS // 2

    for c in range(CHUNKS):
        plus_copy(1, c).start()
        minus_copy(1, c).start()
        if c == 0:
            for k in range(1, ROW):
                row_copy(k).start()

    lane64 = iota((CHIP, 128), 1)
    spacing_x = ((lane64 % CHIP) - iota((CHIP, 128), 0)).astype(F32)
    left64 = lane64 < CHIP
    lane32 = iota((32, 128), 1)
    q32 = lane32 % CHIP
    m32 = 2 * (q32 % 32) + q32 // 32
    spacing_y = (m32 - 2 * iota((32, 128), 0) - lane32 // CHIP).astype(F32)
    left32 = lane32 < CHIP
    decay = -1.0 / (2.0 * SIGMA * SIGMA)

    def prepare(d, carry):
        own = held[0][d]
        for l in range(LINKS):
            i = d * LINKS + l
            off_y = offs_s[0, i].astype(F32) * (1.0 / FIXED)
            off_x = offs_s[1, i].astype(F32) * (1.0 / FIXED)
            tops, bottoms = [], []
            for level in (-1.0, 0.0, 1.0):
                gap = spacing_x - (off_x + level)
                bell = jnp.exp(gap * gap * decay)
                tops.append(jnp.where(left64, bell, 0.0).astype(BF16))
                bottoms.append(jnp.where(left64, 0.0, bell).astype(BF16))
            wide = jnp.concatenate([jnp.concatenate(tops, axis=1), jnp.concatenate(bottoms, axis=1)], axis=0)
            mbuf[i] = jnp.dot(own, wide, preferred_element_type=F32).astype(BF16)
            for e, level in enumerate((-1.0, 0.0, 1.0)):
                gap = spacing_y - (off_y + level)
                lhs[i, pl.ds(32 * e, 32), :] = jnp.exp(gap * gap * decay).astype(BF16)
        return carry

    def prepare_part(n):
        low = sum(PRE[:n])
        lax.fori_loop(low, low + PRE[n], prepare, 0)

    def forward(s, chunks):
        for c in chunks:
            plus_copy(s, c).wait_recv()
            if goes_plus(s + 1, c):
                plus_copy(s + 1, c).start()
            minus_copy(s, c).wait_recv()
            if goes_minus(s + 1, c):
                minus_copy(s + 1, c).start()

    prepare_part(0)
    forward(1, range(2))
    for k in range(1, ROW):
        row_copy(k).wait_recv()
    reqv[pl.ds(0, 8), :] = rowx[pl.ds(8, 8, stride=16), :].astype(jnp.int32)
    reqv[pl.ds(8, 8), :] = jnp.broadcast_to(pair_of, (8, 128)).astype(jnp.int32)
    fetch = pltpu.make_async_copy(reqv, req, sem_req)
    fetch.start()
    forward(1, range(2, CHUNKS))
    fetch.wait()
    total = rowx[pl.ds(0, 8), :]
    for k in range(1, ROW):
        total = total + rowx[pl.ds(16 * k, 8), :]
    zsec[pl.ds(8 * mz, 8), :] = total

    def zsec_copy(k):
        mine = zsec.at[pl.ds(8 * mz, 8)]
        return remote(mine, mine, zsec_s.at[k], zsec_r.at[k], z_peer(k))

    def zsec_arrived(k):
        theirs = zsec.at[pl.ds(8 * lax.rem(mz - k + NZ, NZ), 8)]
        remote(theirs, theirs, zsec_s.at[k], zsec_r.at[k], z_peer(k)).wait_recv()

    def x_copy(g, k):
        first, count = GROUPS[g][0], len(GROUPS[g])
        return remote(
            xsend.at[k, pl.ds(first, count)],
            recv.at[pl.ds(first, count), me],
            x_s.at[g, k],
            x_r.at[g, k],
            row_peer(k),
        )

    def x_arrived(g, k):
        first, count = GROUPS[g][0], len(GROUPS[g])
        theirs = recv.at[pl.ds(first, count), lax.rem(me - k + ROW, ROW)]
        remote(xsend.at[k, pl.ds(first, count)], theirs, x_s.at[g, k], x_r.at[g, k], row_peer(k)).wait_recv()

    def serve(g):
        for k in (4, 3, 5, 2, 6, 1, 7, 0):
            asker = (ROW - k) % ROW
            for t in GROUPS[g]:
                for r in (0, 1):
                    chip = held[t][jnp.clip(req[asker, t * 2 * ROW + me * 2 + r], 0, DATE_DEV - 1)]
                    if k:
                        xsend[k, t, r] = chip
                    else:
                        recv[t, me, r] = chip
            if k:
                x_copy(g, k).start()

    serve(0)
    serve(1)
    for k in range(1, NZ):
        zsec_copy(k).start()
    prepare_part(1)
    for s in (2, 3):
        forward(s, range(CHUNKS))
        serve(s)
        prepare_part(s)
    for c in range(CHUNKS):
        (plus_copy if goes_plus(4, c) else minus_copy)(4, c).wait_recv()
    serve(4)
    prepare_part(4)

    sub8 = iota((8, 128), 0)
    lane8 = iota((8, 128), 1)

    def fold8(parts):
        once = [
            jnp.where(sub8 < 4, parts[j], parts[j + 4])
            + pltpu.roll(jnp.where(sub8 < 4, parts[j + 4], parts[j]), 4, 0)
            for j in range(4)
        ]

        def pair(a, b, n):
            return jnp.where(sub8 % (2 * n) < n, a + pltpu.roll(a, 8 - n, 0), b + pltpu.roll(b, n, 0))

        return pair(pair(once[0], once[2], 2), pair(once[1], once[3], 2), 1)

    def score(t, part):
        slots = [t * 2 * ROW + part * 8 + j for j in range(8)]
        pairs = [jnp.clip(req[8, slot], 0, PAIRS - 1) for slot in slots]
        chip = [recv[t, part * 4 + j // 2, j % 2].astype(F32) for j in range(8)]
        lifted = []
        for j in range(8):
            swapped = pltpu.roll(chip[j], CHIP, 1)
            blocks = jnp.concatenate(
                [
                    jnp.where(left32, chip[j], 0.0).astype(BF16),
                    jnp.where(left32, swapped, 0.0).astype(BF16),
                    jnp.where(left32, 0.0, swapped).astype(BF16),
                    jnp.where(left32, 0.0, chip[j]).astype(BF16),
                ],
                axis=0,
            )
            lifted.append(jnp.dot(lhs[pairs[j]], blocks, preferred_element_type=F32).astype(BF16))
        items = [[] for _ in range(ITEMS)]
        for j in range(8):
            up = lifted[j].astype(F32)
            moved = mbuf[pairs[j]].astype(F32)
            for ky in range(3):
                for kx in range(3):
                    items[3 * ky + kx].append(fold(up[32 * ky : 32 * ky + 32] * moved[:, 128 * kx : 128 * kx + 128]))
            items[9].append(fold(chip[j] * chip[j]))
            items[10].append(bnorm[lax.div(pairs[j], LINKS)])
        table = jnp.zeros((8, 128), F32)
        for item in range(ITEMS):
            table = jnp.where(lane8 == item, jnp.sum(fold8(items[item]), axis=1, keepdims=True), table)
        sums[pl.ds(pl.multiple_of(t * 2 * ROW + part * 8, 8), 8), :] = table

    for g in range(len(GROUPS)):
        for k in range(1, ROW):
            x_arrived(g, k)
        first, count = GROUPS[g][0], len(GROUPS[g])

        def score_step(n, carry, first=first):
            score(first + lax.div(n, 2), lax.rem(n, 2))
            return carry

        lax.fori_loop(0, 2 * count, score_step, 0)

    turned = sums[...].T
    rows = [turned[item : item + 1, :] for item in range(ITEMS)]
    size = CHIP / jnp.sqrt((rows[10] + EPS) * (rows[9] + EPS))
    scores = [rows[q] * size for q in range(9)]
    raised = [jnp.exp(ZSCALE * s) for s in scores]
    whole = raised[0]
    for q in range(1, 9):
        whole = whole + raised[q]
    weights = [r / whole for r in raised]
    shift_y = (weights[6] + weights[7] + weights[8]) - (weights[0] + weights[1] + weights[2])
    shift_x = (weights[2] + weights[5] + weights[8]) - (weights[0] + weights[3] + weights[6])
    blend = weights[0] * scores[0]
    for q in range(1, 9):
        blend = blend + weights[q] * scores[q]
    quality = 1.0 / (1.0 + jnp.exp(-ZSCALE * blend))
    three = jnp.where(sub8 == 0, shift_y, jnp.where(sub8 == 1, shift_x, jnp.where(sub8 == 2, quality, 0.0)))
    chosen = jnp.where(iota((SLOTS, 128), 0).astype(F32) == place_row, 1.0, 0.0).astype(BF16)
    three = thirds_dot(three, chosen)[:, :PAIRS]
    offs = offs_v[...].astype(F32) * (1.0 / FIXED)
    move_y = offs[0:1] + three[0:1]
    move_x = offs[1:2] + three[1:2]
    quality = three[2:3]
    measure_out[0] = move_y
    measure_out[1] = move_x
    measure_out[2] = quality

    up = jnp.where(r8 < 4, jnp.broadcast_to(move_y, (8, PAIRS)), jnp.broadcast_to(move_x, (8, PAIRS)))
    up = jnp.where(ours, up, 0.0)
    down = jnp.where(ours & (r8 < 4), jnp.broadcast_to(quality, (8, PAIRS)), 0.0)
    both = jnp.concatenate([up, down], axis=0)
    mrow[pl.ds(0, 16), :] = thirds_dot(both, deal)

    def mrow_copy(k):
        return remote(mrow.at[pl.ds(0, 16)], mrow.at[pl.ds(16 * k, 16)], mrow_s.at[k], mrow_r.at[k], row_peer(k))

    for k in range(1, ROW):
        mrow_copy(k).start()
    for k in range(1, NZ):
        zsec_arrived(k)

    later = []
    for l in range(LINKS):
        dev = zsec[pl.ds(l, NZ, stride=8), :].astype(jnp.int32)
        pos = zsec[pl.ds(4 + l, NZ, stride=8), :].astype(jnp.int32)
        later.append((dev // ROW, (dev % ROW) * DATE_DEV + pos))
    down128 = iota((128, 128), 0)
    down8 = iota((8, 128), 0)
    for l in range(LINKS):
        for z in range(NZ):
            c = l * NZ + z
            hit = jnp.broadcast_to(later[l][1][z : z + 1, :], (128, 128)) == down128
            onehot[:, pl.ds(128 * c, 128)] = jnp.where(hit, 1.0, 0.0).astype(BF16)
            hit = jnp.broadcast_to(later[l][0][z : z + 1, :], (8, 128)) == down8
            member[pl.ds(8 * c, 8), :] = jnp.where(hit, 1.0, 0.0)
    for k in range(1, ROW):
        mrow_copy(k).wait_recv()
    total = mrow[pl.ds(0, 16), :]
    for k in range(1, ROW):
        total = total + mrow[pl.ds(16 * k, 16), :]
    mall[pl.ds(16 * mz, 16), :] = total

    def mall_copy(k):
        mine = mall.at[pl.ds(16 * mz, 16)]
        return remote(mine, mine, mall_s.at[k], mall_r.at[k], z_peer(k))

    def mall_arrived(k):
        theirs = mall.at[pl.ds(16 * lax.rem(mz - k + NZ, NZ), 16)]
        remote(theirs, theirs, mall_s.at[k], mall_r.at[k], z_peer(k)).wait_recv()

    for k in range(1, NZ):
        mall_copy(k).start()
    for k in range(1, NZ):
        mall_arrived(k)

    meas = [[mall[pl.ds(4 * a + l, NZ, stride=16), :] for l in range(LINKS)] for a in range(2)]
    qual = [mall[pl.ds(8 + l, NZ, stride=16), :] for l in range(LINKS)]
    field = None

    def halo_copy(n, side):
        peer = y_peer((1, ny - 1, 2, ny - 2)[side])
        if n == 0:
            return remote(fsend.at[pl.ds(0, 16)], halo.at[side, pl.ds(0, 16)], halo_s.at[0, side], halo_r.at[0, side], peer)
        return remote(fsend.at[pl.ds(16, 24)], halo.at[side, pl.ds(16, 24)], halo_s.at[1, side], halo_r.at[1, side], peer)

    def inside(steps, value):
        return jnp.where((y + steps >= 0) & (y + steps < ny), value, 0.0)

    def settle(beside, numer, denom):
        return [(LAMBDA * beside[a] + numer[a]) / (2.0 * LAMBDA + denom) for a in range(2)]

    for n, scale in enumerate(MUS):
        square = scale * scale
        numer = [None, None]
        denom = None
        for l in range(LINKS):
            if field is None:
                here = [0.0, 0.0]
                there = [0.0, 0.0]
            else:
                here = field
                there = []
                for a in range(2):
                    got = None
                    for z in range(NZ):
                        table = jnp.broadcast_to(field[a][z : z + 1, :], (NZ, 128))
                        found = jnp.take_along_axis(table, later[l][1], axis=1, mode="promise_in_bounds")
                        got = found if got is None else jnp.where(later[l][0] == z, found, got)
                    there.append(got)
            resid = [meas[a][l] - (there[a] - here[a]) for a in range(2)]
            gnc = qual[l] * square / (square + (resid[0] * resid[0] + resid[1] * resid[1]))
            values = [gnc * (here[a] + meas[a][l]) for a in range(2)] + [gnc]
            for a in range(2):
                back = gnc * (there[a] - meas[a][l])
                numer[a] = back if l == 0 else numer[a] + back
            denom = gnc if l == 0 else denom + gnc
            for z in range(NZ):
                c = l * NZ + z
                mask = member[pl.ds(8 * c, 8), :]
                tall = jnp.concatenate(
                    [jnp.broadcast_to(v[z : z + 1, :], (8, 128)) * mask for v in values], axis=0
                )
                high = tall.astype(BF16)
                low = (tall - high.astype(F32)).astype(BF16)
                spread[:, pl.ds(128 * c, 128)] = jnp.concatenate([high, low], axis=0)
        sent = lax.dot_general(
            spread[...], onehot[...], (((1,), (1,)), ((), ())), preferred_element_type=F32
        )
        sent = sent[0:24] + sent[24:48]
        numer = [numer[a] + sent[8 * a : 8 * a + 8] for a in range(2)]
        denom = denom + sent[16:24]
        if n == 0:
            field = [numer[a] / (2.0 * LAMBDA + denom) for a in range(2)]
            for a in range(2):
                fsend[pl.ds(8 * a, 8), :] = field[a]
            for side in range(4):
                halo_copy(0, side).start()
        elif n == 1:
            for a in range(2):
                fsend[pl.ds(16 + 8 * a, 8), :] = numer[a]
            fsend[pl.ds(32, 8), :] = denom
            for side in (0, 1):
                halo_copy(1, side).start()
            for side in range(4):
                halo_copy(0, side).wait_recv()
            near = [inside(-1, halo[0, pl.ds(8 * a, 8), :]) + inside(1, halo[1, pl.ds(8 * a, 8), :]) for a in range(2)]
            start = field
            field = settle(near, numer, denom)
        else:
            for side in (0, 1):
                halo_copy(1, side).wait_recv()
            beside = [0.0, 0.0]
            for side, way in ((0, -1), (1, 1)):
                reach = [start[a] + inside(2 * way, halo[2 + side, pl.ds(8 * a, 8), :]) for a in range(2)]
                theirs = [halo[side, pl.ds(16 + 8 * a, 8), :] for a in range(2)]
                there = settle(reach, theirs, halo[side, pl.ds(32, 8), :])
                beside = [beside[a] + inside(way, there[a]) for a in range(2)]
            field = settle(beside, numer, denom)

    for a in range(2):
        mine = jnp.sum(jnp.where(down8 == mz, field[a], 0.0), axis=0, keepdims=True)
        turned = pltpu.roll(jnp.broadcast_to(mine, (8, 128)), lax.rem(128 - DATE_DEV * me, 128), 1)
        disp_out[a] = turned[0:1, :DATE_DEV]

    for k in range(1, ROW):
        row_copy(k).wait_send()
        mrow_copy(k).wait_send()
    for k in range(1, NZ):
        zsec_copy(k).wait_send()
        mall_copy(k).wait_send()
    for s in (1, 2, 3, 4):
        for c in range(CHUNKS):
            if goes_plus(s, c):
                plus_copy(s, c).wait_send()
            if goes_minus(s, c):
                minus_copy(s, c).wait_send()
    for g in range(len(GROUPS)):
        for k in range(1, ROW):
            x_copy(g, k).wait_send()
    for n, side in ((0, 0), (0, 1), (0, 2), (0, 3), (1, 0), (1, 1)):
        halo_copy(n, side).wait_send()


def per_device(chips, pair_target, pair_slot, offset_fix):
    flat = chips.reshape(DATE_DEV, CHIP * CHIP)
    target = pair_target.reshape(1, PAIRS)
    slot = pair_slot.reshape(1, PAIRS)
    offs = jnp.transpose(offset_fix.reshape(PAIRS, 2), (1, 0))
    vmem = pl.BlockSpec(memory_space=pltpu.VMEM)
    anywhere = pl.BlockSpec(memory_space=pltpu.HBM)
    dma = pltpu.SemaphoreType.DMA
    measure, disp = pl.pallas_call(
        kernel,
        out_shape=(
            jax.ShapeDtypeStruct((3, 1, PAIRS), F32),
            jax.ShapeDtypeStruct((2, 1, DATE_DEV), F32),
        ),
        in_specs=[anywhere] * 4,
        out_specs=(vmem, vmem),
        scratch_shapes=[
            pltpu.VMEM((DATE_DEV, CHIP * CHIP), BF16),
            pltpu.VMEM((1, PAIRS), jnp.int32),
            pltpu.VMEM((1, PAIRS), jnp.int32),
            pltpu.SMEM((2, PAIRS), jnp.int32),
            pltpu.VMEM((2, PAIRS), jnp.int32),
            pltpu.VMEM((DATE_DEV * 32 + 32, 128), F32),
            *[pltpu.VMEM((DATE_DEV, 32, 128), BF16)] * NZ,
            pltpu.VMEM((ROW, NZ, 2, 32, 128), BF16),
            pltpu.VMEM((NZ, ROW, 2, 32, 128), BF16),
            pltpu.VMEM((DATE_DEV, 8, 128), F32),
            pltpu.VMEM((ROW * 16 + 8, 128), F32),
            pltpu.VMEM((NZ * 8 + 8, 128), F32),
            pltpu.VMEM((16, 128), jnp.int32),
            pltpu.SMEM((16, 128), jnp.int32),
            pltpu.VMEM((PAIRS, 32, 384), BF16),
            pltpu.VMEM((PAIRS, 96, 128), BF16),
            pltpu.VMEM((128, LINKS * NZ * 128), BF16),
            pltpu.VMEM((LINKS * NZ * 8, 128), F32),
            pltpu.VMEM((SLOTS, 128), F32),
            pltpu.VMEM((ROW * 16, 128), F32),
            pltpu.VMEM((NZ * 16 + 16, 128), F32),
            pltpu.VMEM((48, LINKS * NZ * 128), BF16),
            pltpu.VMEM((40, 128), F32),
            pltpu.VMEM((4, 40, 128), F32),
            dma((5,)),
            dma,
            dma((ROW,)),
            dma((ROW,)),
            dma((NZ,)),
            dma((NZ,)),
            dma((4, CHUNKS)),
            dma((4, CHUNKS)),
            dma((4, CHUNKS)),
            dma((4, CHUNKS)),
            dma((len(GROUPS), ROW)),
            dma((len(GROUPS), ROW)),
            dma((ROW,)),
            dma((ROW,)),
            dma((NZ,)),
            dma((NZ,)),
            dma((2, 4)),
            dma((2, 4)),
        ],
        compiler_params=pltpu.CompilerParams(
            collective_id=0, has_side_effects=True, vmem_limit_bytes=40 * 1024 * 1024
        ),
        name="offset_network",
    )(flat, target, slot, offs)
    return (jnp.transpose(disp, (0, 2, 1)), jnp.transpose(measure, (0, 2, 1)))


def solution(mesh):
    in_specs = (P("date", "space", None), P("date", None), P("date"), P("date", "space", None))
    out_specs = (P(None, "date", "space"), P(None, "date", "space"))
    return jax.shard_map(
        per_device, mesh=mesh, in_specs=in_specs, out_specs=out_specs, check_vma=False
    )
```

```python
import jax
import jax.numpy as jnp
from jax import lax
from jax.experimental import pallas as pl
from jax.experimental.pallas import tpu as pltpu
from jax.sharding import PartitionSpec as P

CHIP = 64
LINKS = 4
ROW = 8
FAR_FIRST = (4, 3, 5, 2, 6, 1, 7)
NZ = 8
DATE_DEV = 16
PAIRS = 64
CHUNKS = 4
CHUNK = DATE_DEV // CHUNKS
SIGMA = 0.6
ZSCALE = 0.5
EPS = 1e-06
LAMBDA = 2.0
MUS = (4.0, 2.0, 1.0)
FIXED = 32.0
ITEMS = 10
F32 = jnp.float32
BF16 = jnp.bfloat16
PRE = (9, 2, 2, 3, 0)
SLOTS = 128
GROUPS = ((0,), (1, 2), (3, 4), (5, 6), (7,))


def iota(shape, dim):
    return lax.broadcasted_iota(jnp.int32, shape, dim)


def fold(rows):
    return jnp.sum(rows.reshape(rows.shape[0] // 8, 8, 128), axis=0)


def thirds_dot(value, chosen):
    first = value.astype(BF16)
    rest = value - first.astype(F32)
    second = rest.astype(BF16)
    third = (rest - second.astype(F32)).astype(BF16)
    out = jnp.dot(jnp.concatenate([first, second, third], axis=0), chosen, preferred_element_type=F32)
    n = value.shape[0]
    return out[:n] + out[n : 2 * n] + out[2 * n :]


def kernel(
    chips_in,
    target_in,
    slot_in,
    offs_in,
    measure_out,
    disp_out,
    chips,
    target,
    slot,
    offs_s,
    offs_v,
    tmp,
    held0,
    held1,
    held2,
    held3,
    held4,
    held5,
    held6,
    held7,
    xsend,
    recv,
    bnorm,
    rowx,
    zsec,
    reqv,
    req,
    mbuf,
    lhs,
    onehot,
    member,
    sums,
    mrow,
    mall,
    spread,
    fsend,
    halo,
    sem_in,
    sem_req,
    row_s,
    row_r,
    zsec_s,
    zsec_r,
    plus_s,
    plus_r,
    minus_s,
    minus_r,
    x_s,
    x_r,
    mrow_s,
    mrow_r,
    mall_s,
    mall_r,
    halo_s,
    halo_r,
):
    held = (held0, held1, held2, held3, held4, held5, held6, held7)
    date = lax.axis_index("date")
    y = lax.axis_index("space")
    ny = lax.axis_size("space")
    mz = lax.div(date, ROW)
    me = lax.rem(date, ROW)

    def row_peer(k):
        return {"date": mz * ROW + lax.rem(me + k, ROW)}

    def z_peer(k):
        return {"date": lax.rem(mz + k, NZ) * ROW + me}

    def y_peer(k):
        return {"space": lax.rem(y + k, ny)}

    def remote(src, dst, ssem, rsem, peer):
        return pltpu.make_async_remote_copy(
            src_ref=src,
            dst_ref=dst,
            send_sem=ssem,
            recv_sem=rsem,
            device_id=peer,
            device_id_type=pl.DeviceIdType.MESH,
        )

    barrier = pltpu.get_barrier_semaphore()
    for k in range(1, ROW):
        pl.semaphore_signal(barrier, inc=1, device_id=row_peer(k), device_id_type=pl.DeviceIdType.MESH)
    for k in range(1, NZ):
        pl.semaphore_signal(barrier, inc=1, device_id=z_peer(k), device_id_type=pl.DeviceIdType.MESH)
    for k in (1, 2, ny - 2, ny - 1):
        pl.semaphore_signal(barrier, inc=1, device_id=y_peer(k), device_id_type=pl.DeviceIdType.MESH)

    loads = [
        pltpu.make_async_copy(src, dst, sem_in.at[n])
        for n, (src, dst) in enumerate(
            ((chips_in, chips), (target_in, target), (slot_in, slot), (offs_in, offs_s), (offs_in, offs_v))
        )
    ]
    for load in loads:
        load.start()
    for load in loads[1:]:
        load.wait()

    sub = iota((PAIRS, 128), 0)
    lane = iota((PAIRS, 128), 1)
    zeros64 = jnp.zeros((1, 128 - PAIRS), jnp.int32)
    trow = jnp.concatenate([target[...], zeros64 - 1], axis=1).astype(F32)
    srow = jnp.concatenate([slot[...], zeros64], axis=1).astype(F32)
    tb = jnp.broadcast_to(trow, (PAIRS, 128))
    sb = jnp.broadcast_to(srow, (PAIRS, 128))
    eye = sub == lane
    tcol = jnp.sum(jnp.where(eye, tb, 0.0), axis=1, keepdims=True)
    scol = jnp.sum(jnp.where(eye, sb, 0.0), axis=1, keepdims=True)
    twin = jnp.where((tcol == tb) & (lane < sub), 1.0, 0.0)
    rank = jnp.sum(twin, axis=1, keepdims=True).astype(jnp.int32)
    holder = tcol.astype(jnp.int32)
    away = (holder // ROW - mz + NZ) % NZ
    turn = jnp.where(away < NZ // 2, 2 * away, 2 * NZ - 1 - 2 * away)
    place = turn * (2 * ROW) + (holder % ROW) * 2 + rank
    wanted = jnp.sum(jnp.where(lane == place, scol, 0.0), axis=0, keepdims=True)
    pair_of = jnp.sum(jnp.where(lane == place, sub.astype(F32), 0.0), axis=0, keepdims=True)
    place_row = jnp.sum(jnp.where(eye, place.astype(F32), 0.0), axis=0, keepdims=True)
    deal = jnp.where(lane == me * DATE_DEV + sub // LINKS, 1.0, 0.0).astype(BF16)
    r8 = iota((8, PAIRS), 0)
    l8 = iota((8, PAIRS), 1)
    ours = (l8 % LINKS) == (r8 % LINKS)
    named = jnp.where(r8 < 4, jnp.broadcast_to(trow[:, :PAIRS], (8, PAIRS)), jnp.broadcast_to(srow[:, :PAIRS], (8, PAIRS)))
    named = jnp.where(ours, named, 0.0).astype(BF16)
    rowx[pl.ds(0, 8), :] = jnp.dot(named, deal, preferred_element_type=F32)
    rowx[pl.ds(8, 8), :] = jnp.broadcast_to(wanted, (8, 128))

    loads[0].wait()
    for j in range(32):
        tmp[pl.ds(j, DATE_DEV, stride=32), :] = chips[:, 128 * j : 128 * j + 128].astype(F32)
    for d in range(DATE_DEV):
        own = tmp[pl.ds(32 * d, 32), :]
        held[0][d] = own.astype(BF16)
        bnorm[d] = fold(own * own)

    pl.semaphore_wait(barrier, ROW - 1 + NZ - 1 + 4)

    def row_copy(k):
        return remote(rowx.at[pl.ds(0, 16)], rowx.at[pl.ds(16 * k, 16)], row_s.at[k], row_r.at[k], row_peer(k))

    def ring_part(t, c):
        return held[t].at[pl.ds(c * CHUNK, CHUNK)]

    def plus_copy(s, c):
        return remote(
            ring_part(max(2 * s - 3, 0), c),
            ring_part(2 * s - 1, c),
            plus_s.at[s - 1, c],
            plus_r.at[s - 1, c],
            z_peer(1),
        )

    def minus_copy(s, c):
        return remote(
            ring_part(2 * s - 2, c),
            ring_part(min(2 * s, 7), c),
            minus_s.at[s - 1, c],
            minus_r.at[s - 1, c],
            z_peer(NZ - 1),
        )

    def goes_plus(s, c):
        return s < 4 or c < CHUNKS // 2

    def goes_minus(s, c):
        return s < 4 or c >= CHUNKS // 2

    for c in range(CHUNKS):
        plus_copy(1, c).start()
        minus_copy(1, c).start()
        if c == 0:
            for k in FAR_FIRST:
                row_copy(k).start()

    lane64 = iota((CHIP, 128), 1)
    spacing_x = ((lane64 % CHIP) - iota((CHIP, 128), 0)).astype(F32)
    left64 = lane64 < CHIP
    lane32 = iota((32, 128), 1)
    q32 = lane32 % CHIP
    m32 = 2 * (q32 % 32) + q32 // 32
    spacing_y = (m32 - 2 * iota((32, 128), 0) - lane32 // CHIP).astype(F32)
    left32 = lane32 < CHIP
    decay = -1.0 / (2.0 * SIGMA * SIGMA)

    def prepare(d, carry):
        own = held[0][d]
        for l in range(LINKS):
            i = d * LINKS + l
            off_y = offs_s[0, i].astype(F32) * (1.0 / FIXED)
            off_x = offs_s[1, i].astype(F32) * (1.0 / FIXED)
            tops, bottoms = [], []
            for level in (-1.0, 0.0, 1.0):
                gap = spacing_x - (off_x + level)
                bell = jnp.exp(gap * gap * decay)
                tops.append(jnp.where(left64, bell, 0.0).astype(BF16))
                bottoms.append(jnp.where(left64, 0.0, bell).astype(BF16))
            wide = jnp.concatenate([jnp.concatenate(tops, axis=1), jnp.concatenate(bottoms, axis=1)], axis=0)
            mbuf[i] = jnp.dot(own, wide, preferred_element_type=F32).astype(BF16)
            for e, level in enumerate((-1.0, 0.0, 1.0)):
                gap = spacing_y - (off_y + level)
                lhs[i, pl.ds(32 * e, 32), :] = jnp.exp(gap * gap * decay).astype(BF16)
        return carry

    def prepare_part(n):
        low = sum(PRE[:n])
        lax.fori_loop(low, low + PRE[n], prepare, 0)

    def forward(s, chunks):
        for c in chunks:
            plus_copy(s, c).wait_recv()
            if goes_plus(s + 1, c):
                plus_copy(s + 1, c).start()
            minus_copy(s, c).wait_recv()
            if goes_minus(s + 1, c):
                minus_copy(s + 1, c).start()

    prepare_part(0)
    forward(1, range(2))
    for k in range(1, ROW):
        row_copy(k).wait_recv()
    reqv[pl.ds(0, 8), :] = rowx[pl.ds(8, 8, stride=16), :].astype(jnp.int32)
    reqv[pl.ds(8, 8), :] = jnp.broadcast_to(pair_of, (8, 128)).astype(jnp.int32)
    fetch = pltpu.make_async_copy(reqv, req, sem_req)
    fetch.start()
    forward(1, range(2, CHUNKS))
    fetch.wait()
    total = rowx[pl.ds(0, 8), :]
    for k in range(1, ROW):
        total = total + rowx[pl.ds(16 * k, 8), :]
    zsec[pl.ds(8 * mz, 8), :] = total

    def zsec_copy(k):
        mine = zsec.at[pl.ds(8 * mz, 8)]
        return remote(mine, mine, zsec_s.at[k], zsec_r.at[k], z_peer(k))

    def zsec_arrived(k):
        theirs = zsec.at[pl.ds(8 * lax.rem(mz - k + NZ, NZ), 8)]
        remote(theirs, theirs, zsec_s.at[k], zsec_r.at[k], z_peer(k)).wait_recv()

    def x_copy(g, k):
        first, count = GROUPS[g][0], len(GROUPS[g])
        return remote(
            xsend.at[k, pl.ds(first, count)],
            recv.at[pl.ds(first, count), me],
            x_s.at[g, k],
            x_r.at[g, k],
            row_peer(k),
        )

    def x_arrived(g, k):
        first, count = GROUPS[g][0], len(GROUPS[g])
        theirs = recv.at[pl.ds(first, count), lax.rem(me - k + ROW, ROW)]
        remote(xsend.at[k, pl.ds(first, count)], theirs, x_s.at[g, k], x_r.at[g, k], row_peer(k)).wait_recv()

    def serve(g):
        for k in (4, 3, 5, 2, 6, 1, 7, 0):
            asker = (ROW - k) % ROW
            for t in GROUPS[g]:
                for r in (0, 1):
                    chip = held[t][jnp.clip(req[asker, t * 2 * ROW + me * 2 + r], 0, DATE_DEV - 1)]
                    if k:
                        xsend[k, t, r] = chip
                    else:
                        recv[t, me, r] = chip
            if k:
                x_copy(g, k).start()

    on_left = jnp.where(left32, 1.0, 0.0).astype(BF16)
    on_right = jnp.where(left32, 0.0, 1.0).astype(BF16)
    sub8 = iota((8, 128), 0)
    lane8 = iota((8, 128), 1)

    def fold8(parts):
        once = [
            jnp.where(sub8 < 4, parts[j], parts[j + 4])
            + pltpu.roll(jnp.where(sub8 < 4, parts[j + 4], parts[j]), 4, 0)
            for j in range(4)
        ]

        def pair(a, b, n):
            return jnp.where(sub8 % (2 * n) < n, a + pltpu.roll(a, 8 - n, 0), b + pltpu.roll(b, n, 0))

        return pair(pair(once[0], once[2], 2), pair(once[1], once[3], 2), 1)

    def score(t, part):
        slots = [t * 2 * ROW + part * 8 + j for j in range(8)]
        pairs = [jnp.clip(req[8, slot], 0, PAIRS - 1) for slot in slots]
        chip = [recv[t, part * 4 + j // 2, j % 2].astype(F32) for j in range(8)]
        lifted = []
        for j in range(8):
            swapped = pltpu.roll(chip[j], CHIP, 1).astype(BF16)
            straight = chip[j].astype(BF16)
            blocks = jnp.concatenate(
                [straight * on_left, swapped * on_left, swapped * on_right, straight * on_right], axis=0
            )
            lifted.append(jnp.dot(lhs[pairs[j]], blocks, preferred_element_type=F32).astype(BF16))
        items = [[] for _ in range(ITEMS)]
        for j in range(8):
            up = lifted[j].astype(F32)
            moved = mbuf[pairs[j]].astype(F32)
            for ky in range(3):
                for kx in range(3):
                    items[3 * ky + kx].append(fold(up[32 * ky : 32 * ky + 32] * moved[:, 128 * kx : 128 * kx + 128]))
            items[9].append(fold(chip[j] * chip[j]))
        table = jnp.zeros((8, 128), F32)
        for item in range(ITEMS):
            table = jnp.where(lane8 == item, jnp.sum(fold8(items[item]), axis=1, keepdims=True), table)
        sums[pl.ds(pl.multiple_of(t * 2 * ROW + part * 8, 8), 8), :] = table

    def score_group(g):
        for k in range(1, ROW):
            x_arrived(g, k)
        for t in GROUPS[g]:
            score(t, 0)
            score(t, 1)

    serve(0)
    serve(1)
    prepare_part(1)
    for s in (2, 3):
        forward(s, range(CHUNKS))
        serve(s)
        prepare_part(s)
    for c in range(CHUNKS):
        (plus_copy if goes_plus(4, c) else minus_copy)(4, c).wait_recv()
    serve(4)
    for k in FAR_FIRST:
        zsec_copy(k).start()
    prepare_part(4)

    for g in range(len(GROUPS)):
        score_group(g)

    chosen = jnp.where(iota((SLOTS, 128), 0).astype(F32) == place_row, 1.0, 0.0).astype(BF16)
    rows = thirds_dot(sums[...].T[:16], chosen)[:, :PAIRS]
    rows = [rows[item : item + 1, :] for item in range(ITEMS)]
    norms = jnp.concatenate([fold8([bnorm[8 * h + j] for j in range(8)]) for h in (0, 1)], axis=0)
    norms = jnp.sum(norms, axis=1, keepdims=True)
    leads = iota((DATE_DEV, PAIRS), 0) == iota((DATE_DEV, PAIRS), 1) // LINKS
    rows.append(jnp.sum(jnp.where(leads, norms, 0.0), axis=0, keepdims=True))
    size = CHIP / jnp.sqrt((rows[10] + EPS) * (rows[9] + EPS))
    scores = [rows[q] * size for q in range(9)]
    raised = [jnp.exp(ZSCALE * s) for s in scores]
    whole = raised[0]
    for q in range(1, 9):
        whole = whole + raised[q]
    weights = [r / whole for r in raised]
    shift_y = (weights[6] + weights[7] + weights[8]) - (weights[0] + weights[1] + weights[2])
    shift_x = (weights[2] + weights[5] + weights[8]) - (weights[0] + weights[3] + weights[6])
    blend = weights[0] * scores[0]
    for q in range(1, 9):
        blend = blend + weights[q] * scores[q]
    quality = 1.0 / (1.0 + jnp.exp(-ZSCALE * blend))
    offs = offs_v[...].astype(F32) * (1.0 / FIXED)
    move_y = offs[0:1] + shift_y
    move_x = offs[1:2] + shift_x
    measure_out[0] = move_y
    measure_out[1] = move_x
    measure_out[2] = quality

    up = jnp.where(r8 < 4, jnp.broadcast_to(move_y, (8, PAIRS)), jnp.broadcast_to(move_x, (8, PAIRS)))
    up = jnp.where(ours, up, 0.0)
    down = jnp.where(ours & (r8 < 4), jnp.broadcast_to(quality, (8, PAIRS)), 0.0)
    both = jnp.concatenate([up, down], axis=0)
    mrow[pl.ds(0, 16), :] = thirds_dot(both, deal)

    def mrow_copy(k):
        return remote(mrow.at[pl.ds(0, 16)], mrow.at[pl.ds(16 * k, 16)], mrow_s.at[k], mrow_r.at[k], row_peer(k))

    for k in FAR_FIRST:
        mrow_copy(k).start()
    for k in range(1, NZ):
        zsec_arrived(k)

    later = []
    for l in range(LINKS):
        dev = zsec[pl.ds(l, NZ, stride=8), :].astype(jnp.int32)
        pos = zsec[pl.ds(4 + l, NZ, stride=8), :].astype(jnp.int32)
        later.append((dev // ROW, (dev % ROW) * DATE_DEV + pos))
    across = iota((128, 128), 1).astype(F32)
    down8 = iota((8, 128), 0)
    for l in range(LINKS):
        columns = later[l][1].astype(F32).T
        for z in range(NZ):
            c = l * NZ + z
            hit = columns[:, z : z + 1] == across
            onehot[pl.ds(128 * c, 128), :] = jnp.where(hit, 1.0, 0.0).astype(BF16)
            hit = jnp.broadcast_to(later[l][0][z : z + 1, :], (8, 128)) == down8
            member[pl.ds(8 * c, 8), :] = jnp.where(hit, 1.0, 0.0)
    for k in range(1, ROW):
        mrow_copy(k).wait_recv()
    total = mrow[pl.ds(0, 16), :]
    for k in range(1, ROW):
        total = total + mrow[pl.ds(16 * k, 16), :]
    mall[pl.ds(16 * mz, 16), :] = total

    def mall_copy(k):
        mine = mall.at[pl.ds(16 * mz, 16)]
        return remote(mine, mine, mall_s.at[k], mall_r.at[k], z_peer(k))

    def mall_arrived(k):
        theirs = mall.at[pl.ds(16 * lax.rem(mz - k + NZ, NZ), 16)]
        remote(theirs, theirs, mall_s.at[k], mall_r.at[k], z_peer(k)).wait_recv()

    for k in FAR_FIRST:
        mall_copy(k).start()
    for k in range(1, NZ):
        mall_arrived(k)

    meas = [[mall[pl.ds(4 * a + l, NZ, stride=16), :] for l in range(LINKS)] for a in range(2)]
    qual = [mall[pl.ds(8 + l, NZ, stride=16), :] for l in range(LINKS)]
    field = None

    def halo_copy(n, side):
        peer = y_peer((1, ny - 1, 2, ny - 2)[side])
        if n == 0:
            return remote(fsend.at[pl.ds(0, 16)], halo.at[side, pl.ds(0, 16)], halo_s.at[0, side], halo_r.at[0, side], peer)
        return remote(fsend.at[pl.ds(16, 24)], halo.at[side, pl.ds(16, 24)], halo_s.at[1, side], halo_r.at[1, side], peer)

    def inside(steps, value):
        return jnp.where((y + steps >= 0) & (y + steps < ny), value, 0.0)

    def settle(beside, numer, denom):
        return [(LAMBDA * beside[a] + numer[a]) / (2.0 * LAMBDA + denom) for a in range(2)]

    for n, scale in enumerate(MUS):
        square = scale * scale
        numer = [None, None]
        denom = None
        for l in range(LINKS):
            if field is None:
                here = [0.0, 0.0]
                there = [0.0, 0.0]
            else:
                here = field
                there = []
                for a in range(2):
                    got = None
                    for z in range(NZ):
                        table = jnp.broadcast_to(field[a][z : z + 1, :], (NZ, 128))
                        found = jnp.take_along_axis(table, later[l][1], axis=1, mode="promise_in_bounds")
                        got = found if got is None else jnp.where(later[l][0] == z, found, got)
                    there.append(got)
            resid = [meas[a][l] - (there[a] - here[a]) for a in range(2)]
            gnc = qual[l] * square / (square + (resid[0] * resid[0] + resid[1] * resid[1]))
            values = [gnc * (here[a] + meas[a][l]) for a in range(2)] + [gnc]
            for a in range(2):
                back = gnc * (there[a] - meas[a][l])
                numer[a] = back if l == 0 else numer[a] + back
            denom = gnc if l == 0 else denom + gnc
            for z in range(NZ):
                c = l * NZ + z
                mask = member[pl.ds(8 * c, 8), :]
                tall = jnp.concatenate(
                    [jnp.broadcast_to(v[z : z + 1, :], (8, 128)) * mask for v in values], axis=0
                )
                high = tall.astype(BF16)
                low = (tall - high.astype(F32)).astype(BF16)
                spread[:, pl.ds(128 * c, 128)] = jnp.concatenate([high, low], axis=0)
        sent = lax.dot_general(
            spread[...], onehot[...], (((1,), (0,)), ((), ())), preferred_element_type=F32
        )
        sent = sent[0:24] + sent[24:48]
        numer = [numer[a] + sent[8 * a : 8 * a + 8] for a in range(2)]
        denom = denom + sent[16:24]
        if n == 0:
            field = [numer[a] / (2.0 * LAMBDA + denom) for a in range(2)]
            for a in range(2):
                fsend[pl.ds(8 * a, 8), :] = field[a]
            for side in (2, 3, 0, 1):
                halo_copy(0, side).start()
        elif n == 1:
            for a in range(2):
                fsend[pl.ds(16 + 8 * a, 8), :] = numer[a]
            fsend[pl.ds(32, 8), :] = denom
            for side in (0, 1):
                halo_copy(1, side).start()
            for side in range(4):
                halo_copy(0, side).wait_recv()
            near = [inside(-1, halo[0, pl.ds(8 * a, 8), :]) + inside(1, halo[1, pl.ds(8 * a, 8), :]) for a in range(2)]
            start = field
            field = settle(near, numer, denom)
        else:
            for side in (0, 1):
                halo_copy(1, side).wait_recv()
            beside = [0.0, 0.0]
            for side, way in ((0, -1), (1, 1)):
                reach = [start[a] + inside(2 * way, halo[2 + side, pl.ds(8 * a, 8), :]) for a in range(2)]
                theirs = [halo[side, pl.ds(16 + 8 * a, 8), :] for a in range(2)]
                there = settle(reach, theirs, halo[side, pl.ds(32, 8), :])
                beside = [beside[a] + inside(way, there[a]) for a in range(2)]
            field = settle(beside, numer, denom)

    for a in range(2):
        mine = jnp.sum(jnp.where(down8 == mz, field[a], 0.0), axis=0, keepdims=True)
        turned = pltpu.roll(jnp.broadcast_to(mine, (8, 128)), lax.rem(128 - DATE_DEV * me, 128), 1)
        disp_out[a] = turned[0:1, :DATE_DEV]

    for k in range(1, ROW):
        row_copy(k).wait_send()
        mrow_copy(k).wait_send()
    for k in range(1, NZ):
        zsec_copy(k).wait_send()
        mall_copy(k).wait_send()
    for s in (1, 2, 3, 4):
        for c in range(CHUNKS):
            if goes_plus(s, c):
                plus_copy(s, c).wait_send()
            if goes_minus(s, c):
                minus_copy(s, c).wait_send()
    for g in range(len(GROUPS)):
        for k in range(1, ROW):
            x_copy(g, k).wait_send()
    for n, side in ((0, 0), (0, 1), (0, 2), (0, 3), (1, 0), (1, 1)):
        halo_copy(n, side).wait_send()


def per_device(chips, pair_target, pair_slot, offset_fix):
    flat = chips.reshape(DATE_DEV, CHIP * CHIP)
    target = pair_target.reshape(1, PAIRS)
    slot = pair_slot.reshape(1, PAIRS)
    offs = jnp.transpose(offset_fix.reshape(PAIRS, 2), (1, 0))
    vmem = pl.BlockSpec(memory_space=pltpu.VMEM)
    anywhere = pl.BlockSpec(memory_space=pltpu.HBM)
    dma = pltpu.SemaphoreType.DMA
    measure, disp = pl.pallas_call(
        kernel,
        out_shape=(
            jax.ShapeDtypeStruct((3, 1, PAIRS), F32),
            jax.ShapeDtypeStruct((2, 1, DATE_DEV), F32),
        ),
        in_specs=[anywhere] * 4,
        out_specs=(vmem, vmem),
        scratch_shapes=[
            pltpu.VMEM((DATE_DEV, CHIP * CHIP), BF16),
            pltpu.VMEM((1, PAIRS), jnp.int32),
            pltpu.VMEM((1, PAIRS), jnp.int32),
            pltpu.SMEM((2, PAIRS), jnp.int32),
            pltpu.VMEM((2, PAIRS), jnp.int32),
            pltpu.VMEM((DATE_DEV * 32 + 32, 128), F32),
            *[pltpu.VMEM((DATE_DEV, 32, 128), BF16)] * NZ,
            pltpu.VMEM((ROW, NZ, 2, 32, 128), BF16),
            pltpu.VMEM((NZ, ROW, 2, 32, 128), BF16),
            pltpu.VMEM((DATE_DEV, 8, 128), F32),
            pltpu.VMEM((ROW * 16 + 8, 128), F32),
            pltpu.VMEM((NZ * 8 + 8, 128), F32),
            pltpu.VMEM((16, 128), jnp.int32),
            pltpu.SMEM((16, 128), jnp.int32),
            pltpu.VMEM((PAIRS, 32, 384), BF16),
            pltpu.VMEM((PAIRS, 96, 128), BF16),
            pltpu.VMEM((LINKS * NZ * 128, 128), BF16),
            pltpu.VMEM((LINKS * NZ * 8, 128), F32),
            pltpu.VMEM((SLOTS, 128), F32),
            pltpu.VMEM((ROW * 16, 128), F32),
            pltpu.VMEM((NZ * 16 + 16, 128), F32),
            pltpu.VMEM((48, LINKS * NZ * 128), BF16),
            pltpu.VMEM((40, 128), F32),
            pltpu.VMEM((4, 40, 128), F32),
            dma((5,)),
            dma,
            dma((ROW,)),
            dma((ROW,)),
            dma((NZ,)),
            dma((NZ,)),
            dma((4, CHUNKS)),
            dma((4, CHUNKS)),
            dma((4, CHUNKS)),
            dma((4, CHUNKS)),
            dma((len(GROUPS), ROW)),
            dma((len(GROUPS), ROW)),
            dma((ROW,)),
            dma((ROW,)),
            dma((NZ,)),
            dma((NZ,)),
            dma((2, 4)),
            dma((2, 4)),
        ],
        compiler_params=pltpu.CompilerParams(
            collective_id=0, has_side_effects=True, vmem_limit_bytes=40 * 1024 * 1024
        ),
        name="offset_network",
    )(flat, target, slot, offs)
    return (jnp.transpose(disp, (0, 2, 1)), jnp.transpose(measure, (0, 2, 1)))


def solution(mesh):
    in_specs = (P("date", "space", None), P("date", None), P("date"), P("date", "space", None))
    out_specs = (P(None, "date", "space"), P(None, "date", "space"))
    return jax.shard_map(
        per_device, mesh=mesh, in_specs=in_specs, out_specs=out_specs, check_vma=False
    )
```

```python
import jax
import jax.numpy as jnp
from jax import lax
from jax.experimental import pallas as pl
from jax.experimental.pallas import tpu as pltpu
from jax.sharding import PartitionSpec as P

CHIP = 64
LINKS = 4
ROW = 8
FAR_FIRST = (4, 3, 5, 2, 6, 1, 7)
NZ = 8
DATE_DEV = 16
PAIRS = 64
CHUNKS = 4
CHUNK = DATE_DEV // CHUNKS
SIGMA = 0.6
ZSCALE = 0.5
EPS = 1e-06
LAMBDA = 2.0
MUS = (4.0, 2.0, 1.0)
FIXED = 32.0
ITEMS = 10
F32 = jnp.float32
BF16 = jnp.bfloat16
PRE = (9, 2, 2, 3, 0)
SLOTS = 128
GROUPS = ((0,), (1, 2), (3, 4), (5, 6), (7,))


def iota(shape, dim):
    return lax.broadcasted_iota(jnp.int32, shape, dim)


def fold(rows):
    return jnp.sum(rows.reshape(rows.shape[0] // 8, 8, 128), axis=0)


def thirds_dot(value, chosen):
    first = value.astype(BF16)
    rest = value - first.astype(F32)
    second = rest.astype(BF16)
    third = (rest - second.astype(F32)).astype(BF16)
    out = jnp.dot(jnp.concatenate([first, second, third], axis=0), chosen, preferred_element_type=F32)
    n = value.shape[0]
    return out[:n] + out[n : 2 * n] + out[2 * n :]


def kernel(
    chips_in,
    target_in,
    slot_in,
    offs_in,
    measure_out,
    disp_out,
    chips,
    target,
    slot,
    offs_s,
    offs_v,
    tmp,
    held0,
    held1,
    held2,
    held3,
    held4,
    held5,
    held6,
    held7,
    xsend,
    recv,
    bnorm,
    rowx,
    zsec,
    reqv,
    req,
    mbuf,
    lhs,
    onehot,
    member,
    sums,
    mrow,
    mall,
    spread,
    fsend,
    halo,
    sem_in,
    sem_req,
    row_s,
    row_r,
    zsec_s,
    zsec_r,
    plus_s,
    plus_r,
    minus_s,
    minus_r,
    x_s,
    x_r,
    mrow_s,
    mrow_r,
    mall_s,
    mall_r,
    halo_s,
    halo_r,
):
    held = (held0, held1, held2, held3, held4, held5, held6, held7)
    date = lax.axis_index("date")
    y = lax.axis_index("space")
    ny = lax.axis_size("space")
    mz = lax.div(date, ROW)
    me = lax.rem(date, ROW)

    def row_peer(k):
        return {"date": mz * ROW + lax.rem(me + k, ROW)}

    def z_peer(k):
        return {"date": lax.rem(mz + k, NZ) * ROW + me}

    def y_peer(k):
        return {"space": lax.rem(y + k, ny)}

    def remote(src, dst, ssem, rsem, peer):
        return pltpu.make_async_remote_copy(
            src_ref=src,
            dst_ref=dst,
            send_sem=ssem,
            recv_sem=rsem,
            device_id=peer,
            device_id_type=pl.DeviceIdType.MESH,
        )

    barrier = pltpu.get_barrier_semaphore()
    for k in range(1, ROW):
        pl.semaphore_signal(barrier, inc=1, device_id=row_peer(k), device_id_type=pl.DeviceIdType.MESH)
    for k in range(1, NZ):
        pl.semaphore_signal(barrier, inc=1, device_id=z_peer(k), device_id_type=pl.DeviceIdType.MESH)
    for k in (1, 2, ny - 2, ny - 1):
        pl.semaphore_signal(barrier, inc=1, device_id=y_peer(k), device_id_type=pl.DeviceIdType.MESH)

    loads = [
        pltpu.make_async_copy(src, dst, sem_in.at[n])
        for n, (src, dst) in enumerate(
            ((chips_in, chips), (target_in, target), (slot_in, slot), (offs_in, offs_s), (offs_in, offs_v))
        )
    ]
    for load in loads:
        load.start()
    for load in loads[1:]:
        load.wait()

    sub = iota((PAIRS, 128), 0)
    lane = iota((PAIRS, 128), 1)
    zeros64 = jnp.zeros((1, 128 - PAIRS), jnp.int32)
    trow = jnp.concatenate([target[...], zeros64 - 1], axis=1).astype(F32)
    srow = jnp.concatenate([slot[...], zeros64], axis=1).astype(F32)
    tb = jnp.broadcast_to(trow, (PAIRS, 128))
    sb = jnp.broadcast_to(srow, (PAIRS, 128))
    eye = sub == lane
    tcol = jnp.sum(jnp.where(eye, tb, 0.0), axis=1, keepdims=True)
    scol = jnp.sum(jnp.where(eye, sb, 0.0), axis=1, keepdims=True)
    twin = jnp.where((tcol == tb) & (lane < sub), 1.0, 0.0)
    rank = jnp.sum(twin, axis=1, keepdims=True).astype(jnp.int32)
    holder = tcol.astype(jnp.int32)
    away = (holder // ROW - mz + NZ) % NZ
    turn = jnp.where(away < NZ // 2, 2 * away, 2 * NZ - 1 - 2 * away)
    place = turn * (2 * ROW) + (holder % ROW) * 2 + rank
    wanted = jnp.sum(jnp.where(lane == place, scol, 0.0), axis=0, keepdims=True)
    pair_of = jnp.sum(jnp.where(lane == place, sub.astype(F32), 0.0), axis=0, keepdims=True)
    place_row = jnp.sum(jnp.where(eye, place.astype(F32), 0.0), axis=0, keepdims=True)
    deal = jnp.where(lane == me * DATE_DEV + sub // LINKS, 1.0, 0.0).astype(BF16)
    r8 = iota((8, PAIRS), 0)
    l8 = iota((8, PAIRS), 1)
    ours = (l8 % LINKS) == (r8 % LINKS)
    named = jnp.where(r8 < 4, jnp.broadcast_to(trow[:, :PAIRS], (8, PAIRS)), jnp.broadcast_to(srow[:, :PAIRS], (8, PAIRS)))
    named = jnp.where(ours, named, 0.0).astype(BF16)
    rowx[pl.ds(0, 8), :] = jnp.dot(named, deal, preferred_element_type=F32)
    rowx[pl.ds(8, 8), :] = jnp.broadcast_to(wanted, (8, 128))

    loads[0].wait()
    for j in range(32):
        tmp[pl.ds(j, DATE_DEV, stride=32), :] = chips[:, 128 * j : 128 * j + 128].astype(F32)
    for d in range(DATE_DEV):
        own = tmp[pl.ds(32 * d, 32), :]
        held[0][d] = own.astype(BF16)
        bnorm[d] = fold(own * own)

    pl.semaphore_wait(barrier, ROW - 1 + NZ - 1 + 4)

    def row_copy(k):
        return remote(rowx.at[pl.ds(0, 16)], rowx.at[pl.ds(16 * k, 16)], row_s.at[k], row_r.at[k], row_peer(k))

    def ring_part(t, c):
        return held[t].at[pl.ds(c * CHUNK, CHUNK)]

    def plus_copy(s, c):
        return remote(
            ring_part(max(2 * s - 3, 0), c),
            ring_part(2 * s - 1, c),
            plus_s.at[s - 1, c],
            plus_r.at[s - 1, c],
            z_peer(1),
        )

    def minus_copy(s, c):
        return remote(
            ring_part(2 * s - 2, c),
            ring_part(min(2 * s, 7), c),
            minus_s.at[s - 1, c],
            minus_r.at[s - 1, c],
            z_peer(NZ - 1),
        )

    def goes_plus(s, c):
        return s < 4 or c < CHUNKS // 2

    def goes_minus(s, c):
        return s < 4 or c >= CHUNKS // 2

    for c in range(CHUNKS):
        plus_copy(1, c).start()
        minus_copy(1, c).start()
        if c == 0:
            for k in FAR_FIRST:
                row_copy(k).start()

    lane64 = iota((CHIP, 128), 1)
    spacing_x = ((lane64 % CHIP) - iota((CHIP, 128), 0)).astype(F32)
    left64 = lane64 < CHIP
    lane32 = iota((32, 128), 1)
    q32 = lane32 % CHIP
    m32 = 2 * (q32 % 32) + q32 // 32
    spacing_y = (m32 - 2 * iota((32, 128), 0) - lane32 // CHIP).astype(F32)
    left32 = lane32 < CHIP
    decay = -1.0 / (2.0 * SIGMA * SIGMA)

    def prepare(d, carry):
        own = held[0][d]
        for l in range(LINKS):
            i = d * LINKS + l
            off_y = offs_s[0, i].astype(F32) * (1.0 / FIXED)
            off_x = offs_s[1, i].astype(F32) * (1.0 / FIXED)
            tops, bottoms = [], []
            for level in (-1.0, 0.0, 1.0):
                gap = spacing_x - (off_x + level)
                bell = jnp.exp(gap * gap * decay)
                tops.append(jnp.where(left64, bell, 0.0).astype(BF16))
                bottoms.append(jnp.where(left64, 0.0, bell).astype(BF16))
            wide = jnp.concatenate([jnp.concatenate(tops, axis=1), jnp.concatenate(bottoms, axis=1)], axis=0)
            mbuf[i] = jnp.dot(own, wide, preferred_element_type=F32).astype(BF16)
            for e, level in enumerate((-1.0, 0.0, 1.0)):
                gap = spacing_y - (off_y + level)
                lhs[i, pl.ds(32 * e, 32), :] = jnp.exp(gap * gap * decay).astype(BF16)
        return carry

    def prepare_part(n):
        low = sum(PRE[:n])
        lax.fori_loop(low, low + PRE[n], prepare, 0)

    def forward(s, chunks):
        for c in chunks:
            plus_copy(s, c).wait_recv()
            if goes_plus(s + 1, c):
                plus_copy(s + 1, c).start()
            minus_copy(s, c).wait_recv()
            if goes_minus(s + 1, c):
                minus_copy(s + 1, c).start()

    prepare_part(0)
    forward(1, range(2))
    for k in range(1, ROW):
        row_copy(k).wait_recv()
    reqv[pl.ds(0, 8), :] = rowx[pl.ds(8, 8, stride=16), :].astype(jnp.int32)
    reqv[pl.ds(8, 8), :] = jnp.broadcast_to(pair_of, (8, 128)).astype(jnp.int32)
    fetch = pltpu.make_async_copy(reqv, req, sem_req)
    fetch.start()
    forward(1, range(2, CHUNKS))
    fetch.wait()
    total = rowx[pl.ds(0, 8), :]
    for k in range(1, ROW):
        total = total + rowx[pl.ds(16 * k, 8), :]
    zsec[pl.ds(8 * mz, 8), :] = total

    def zsec_copy(k):
        mine = zsec.at[pl.ds(8 * mz, 8)]
        return remote(mine, mine, zsec_s.at[k], zsec_r.at[k], z_peer(k))

    def zsec_arrived(k):
        theirs = zsec.at[pl.ds(8 * lax.rem(mz - k + NZ, NZ), 8)]
        remote(theirs, theirs, zsec_s.at[k], zsec_r.at[k], z_peer(k)).wait_recv()

    def x_copy(g, k):
        first, count = GROUPS[g][0], len(GROUPS[g])
        return remote(
            xsend.at[k, pl.ds(first, count)],
            recv.at[pl.ds(first, count), me],
            x_s.at[g, k],
            x_r.at[g, k],
            row_peer(k),
        )

    def x_arrived(g, k):
        first, count = GROUPS[g][0], len(GROUPS[g])
        theirs = recv.at[pl.ds(first, count), lax.rem(me - k + ROW, ROW)]
        remote(xsend.at[k, pl.ds(first, count)], theirs, x_s.at[g, k], x_r.at[g, k], row_peer(k)).wait_recv()

    def serve(g):
        for k in (4, 3, 5, 2, 6, 1, 7, 0):
            asker = (ROW - k) % ROW
            for t in GROUPS[g]:
                for r in (0, 1):
                    chip = held[t][jnp.clip(req[asker, t * 2 * ROW + me * 2 + r], 0, DATE_DEV - 1)]
                    if k:
                        xsend[k, t, r] = chip
                    else:
                        recv[t, me, r] = chip
            if k:
                x_copy(g, k).start()

    on_left = jnp.where(left32, 1.0, 0.0).astype(BF16)
    on_right = jnp.where(left32, 0.0, 1.0).astype(BF16)
    sub8 = iota((8, 128), 0)
    lane8 = iota((8, 128), 1)

    def fold8(parts):
        once = [
            jnp.where(sub8 < 4, parts[j], parts[j + 4])
            + pltpu.roll(jnp.where(sub8 < 4, parts[j + 4], parts[j]), 4, 0)
            for j in range(4)
        ]

        def pair(a, b, n):
            return jnp.where(sub8 % (2 * n) < n, a + pltpu.roll(a, 8 - n, 0), b + pltpu.roll(b, n, 0))

        return pair(pair(once[0], once[2], 2), pair(once[1], once[3], 2), 1)

    def score(t, part):
        slots = [t * 2 * ROW + part * 8 + j for j in range(8)]
        pairs = [jnp.clip(req[8, slot], 0, PAIRS - 1) for slot in slots]
        chip = [recv[t, part * 4 + j // 2, j % 2].astype(F32) for j in range(8)]
        lifted = []
        for j in range(8):
            swapped = pltpu.roll(chip[j], CHIP, 1).astype(BF16)
            straight = chip[j].astype(BF16)
            blocks = jnp.concatenate(
                [straight * on_left, swapped * on_left, swapped * on_right, straight * on_right], axis=0
            )
            lifted.append(jnp.dot(lhs[pairs[j]], blocks, preferred_element_type=F32).astype(BF16))
        items = [[] for _ in range(ITEMS)]
        for j in range(8):
            up = lifted[j].astype(F32)
            moved = mbuf[pairs[j]].astype(F32)
            for ky in range(3):
                for kx in range(3):
                    items[3 * ky + kx].append(fold(up[32 * ky : 32 * ky + 32] * moved[:, 128 * kx : 128 * kx + 128]))
            items[9].append(fold(chip[j] * chip[j]))
        table = jnp.zeros((8, 128), F32)
        for item in range(ITEMS):
            table = jnp.where(lane8 == item, jnp.sum(fold8(items[item]), axis=1, keepdims=True), table)
        sums[pl.ds(pl.multiple_of(t * 2 * ROW + part * 8, 8), 8), :] = table

    def score_group(g):
        for k in range(1, ROW):
            x_arrived(g, k)
        for t in GROUPS[g]:
            score(t, 0)
            score(t, 1)

    serve(0)
    serve(1)
    prepare_part(1)
    for s in (2, 3):
        forward(s, range(CHUNKS))
        serve(s)
        prepare_part(s)
    for c in range(CHUNKS):
        (plus_copy if goes_plus(4, c) else minus_copy)(4, c).wait_recv()
    serve(4)
    for k in FAR_FIRST:
        zsec_copy(k).start()
    prepare_part(4)

    for g in range(len(GROUPS)):
        score_group(g)

    chosen = jnp.where(iota((SLOTS, 128), 0).astype(F32) == place_row, 1.0, 0.0).astype(BF16)
    rows = thirds_dot(sums[...].T[:16], chosen)[:, :PAIRS]
    rows = [rows[item : item + 1, :] for item in range(ITEMS)]
    norms = jnp.concatenate([fold8([bnorm[8 * h + j] for j in range(8)]) for h in (0, 1)], axis=0)
    norms = jnp.sum(norms, axis=1, keepdims=True)
    leads = iota((DATE_DEV, PAIRS), 0) == iota((DATE_DEV, PAIRS), 1) // LINKS
    rows.append(jnp.sum(jnp.where(leads, norms, 0.0), axis=0, keepdims=True))
    size = CHIP / jnp.sqrt((rows[10] + EPS) * (rows[9] + EPS))
    scores = [rows[q] * size for q in range(9)]
    raised = [jnp.exp(ZSCALE * s) for s in scores]
    whole = raised[0]
    for q in range(1, 9):
        whole = whole + raised[q]
    weights = [r / whole for r in raised]
    shift_y = (weights[6] + weights[7] + weights[8]) - (weights[0] + weights[1] + weights[2])
    shift_x = (weights[2] + weights[5] + weights[8]) - (weights[0] + weights[3] + weights[6])
    blend = weights[0] * scores[0]
    for q in range(1, 9):
        blend = blend + weights[q] * scores[q]
    quality = 1.0 / (1.0 + jnp.exp(-ZSCALE * blend))
    offs = offs_v[...].astype(F32) * (1.0 / FIXED)
    move_y = offs[0:1] + shift_y
    move_x = offs[1:2] + shift_x
    measure_out[0] = move_y
    measure_out[1] = move_x
    measure_out[2] = quality

    up = jnp.where(r8 < 4, jnp.broadcast_to(move_y, (8, PAIRS)), jnp.broadcast_to(move_x, (8, PAIRS)))
    up = jnp.where(ours, up, 0.0)
    down = jnp.where(ours & (r8 < 4), jnp.broadcast_to(quality, (8, PAIRS)), 0.0)
    both = jnp.concatenate([up, down], axis=0)
    mrow[pl.ds(0, 16), :] = thirds_dot(both, deal)

    def mrow_copy(k):
        return remote(mrow.at[pl.ds(0, 16)], mrow.at[pl.ds(16 * k, 16)], mrow_s.at[k], mrow_r.at[k], row_peer(k))

    for k in FAR_FIRST:
        mrow_copy(k).start()
    for k in range(1, NZ):
        zsec_arrived(k)

    later = []
    for l in range(LINKS):
        dev = zsec[pl.ds(l, NZ, stride=8), :].astype(jnp.int32)
        pos = zsec[pl.ds(4 + l, NZ, stride=8), :].astype(jnp.int32)
        later.append((dev // ROW, (dev % ROW) * DATE_DEV + pos))
    across = iota((128, 128), 1).astype(F32)
    down8 = iota((8, 128), 0)
    for l in range(LINKS):
        columns = later[l][1].astype(F32).T
        for z in range(NZ):
            c = l * NZ + z
            hit = columns[:, z : z + 1] == across
            onehot[pl.ds(128 * c, 128), :] = jnp.where(hit, 1.0, 0.0).astype(BF16)
            hit = jnp.broadcast_to(later[l][0][z : z + 1, :], (8, 128)) == down8
            member[pl.ds(8 * c, 8), :] = jnp.where(hit, 1.0, 0.0)
    for k in range(1, ROW):
        mrow_copy(k).wait_recv()
    total = mrow[pl.ds(0, 16), :]
    for k in range(1, ROW):
        total = total + mrow[pl.ds(16 * k, 16), :]
    mall[pl.ds(16 * mz, 16), :] = total

    def mall_copy(k):
        mine = mall.at[pl.ds(16 * mz, 16)]
        return remote(mine, mine, mall_s.at[k], mall_r.at[k], z_peer(k))

    def mall_arrived(k):
        theirs = mall.at[pl.ds(16 * lax.rem(mz - k + NZ, NZ), 16)]
        remote(theirs, theirs, mall_s.at[k], mall_r.at[k], z_peer(k)).wait_recv()

    for k in FAR_FIRST:
        mall_copy(k).start()
    for k in range(1, NZ):
        mall_arrived(k)

    meas = [[mall[pl.ds(4 * a + l, NZ, stride=16), :] for l in range(LINKS)] for a in range(2)]
    qual = [mall[pl.ds(8 + l, NZ, stride=16), :] for l in range(LINKS)]
    field = None

    def halo_copy(n, side):
        peer = y_peer((1, ny - 1, 2, ny - 2)[side])
        if n == 0:
            return remote(fsend.at[pl.ds(0, 16)], halo.at[side, pl.ds(0, 16)], halo_s.at[0, side], halo_r.at[0, side], peer)
        return remote(fsend.at[pl.ds(16, 24)], halo.at[side, pl.ds(16, 24)], halo_s.at[1, side], halo_r.at[1, side], peer)

    def inside(steps, value):
        return jnp.where((y + steps >= 0) & (y + steps < ny), value, 0.0)

    def settle(beside, numer, denom):
        return [(LAMBDA * beside[a] + numer[a]) / (2.0 * LAMBDA + denom) for a in range(2)]

    for n, scale in enumerate(MUS):
        square = scale * scale
        numer = [None, None]
        denom = None
        for l in range(LINKS):
            if field is None:
                here = [0.0, 0.0]
                there = [0.0, 0.0]
            else:
                here = field
                there = []
                for a in range(2):
                    got = None
                    for z in range(NZ):
                        table = jnp.broadcast_to(field[a][z : z + 1, :], (NZ, 128))
                        found = jnp.take_along_axis(table, later[l][1], axis=1, mode="promise_in_bounds")
                        got = found if got is None else jnp.where(later[l][0] == z, found, got)
                    there.append(got)
            resid = [meas[a][l] - (there[a] - here[a]) for a in range(2)]
            gnc = qual[l] * square / (square + (resid[0] * resid[0] + resid[1] * resid[1]))
            values = [gnc * (here[a] + meas[a][l]) for a in range(2)] + [gnc]
            for a in range(2):
                back = gnc * (there[a] - meas[a][l])
                numer[a] = back if l == 0 else numer[a] + back
            denom = gnc if l == 0 else denom + gnc
            for z in range(NZ):
                c = l * NZ + z
                mask = member[pl.ds(8 * c, 8), :]
                tall = jnp.concatenate(
                    [jnp.broadcast_to(v[z : z + 1, :], (8, 128)) * mask for v in values], axis=0
                )
                high = tall.astype(BF16)
                low = (tall - high.astype(F32)).astype(BF16)
                spread[:, pl.ds(128 * c, 128)] = jnp.concatenate([high, low], axis=0)
        sent = lax.dot_general(
            spread[...], onehot[...], (((1,), (0,)), ((), ())), preferred_element_type=F32
        )
        sent = sent[0:24] + sent[24:48]
        numer = [numer[a] + sent[8 * a : 8 * a + 8] for a in range(2)]
        denom = denom + sent[16:24]
        if n == 0:
            field = [numer[a] / (2.0 * LAMBDA + denom) for a in range(2)]
            for a in range(2):
                fsend[pl.ds(8 * a, 8), :] = field[a]
            for side in (2, 3, 0, 1):
                halo_copy(0, side).start()
        elif n == 1:
            for a in range(2):
                fsend[pl.ds(16 + 8 * a, 8), :] = numer[a]
            fsend[pl.ds(32, 8), :] = denom
            for side in (0, 1):
                halo_copy(1, side).start()
            for side in range(4):
                halo_copy(0, side).wait_recv()
            near = [inside(-1, halo[0, pl.ds(8 * a, 8), :]) + inside(1, halo[1, pl.ds(8 * a, 8), :]) for a in range(2)]
            start = field
            field = settle(near, numer, denom)
        else:
            for side in (0, 1):
                halo_copy(1, side).wait_recv()
            beside = [0.0, 0.0]
            for side, way in ((0, -1), (1, 1)):
                reach = [start[a] + inside(2 * way, halo[2 + side, pl.ds(8 * a, 8), :]) for a in range(2)]
                theirs = [halo[side, pl.ds(16 + 8 * a, 8), :] for a in range(2)]
                there = settle(reach, theirs, halo[side, pl.ds(32, 8), :])
                beside = [beside[a] + inside(way, there[a]) for a in range(2)]
            field = settle(beside, numer, denom)

    for a in range(2):
        mine = jnp.sum(jnp.where(down8 == mz, field[a], 0.0), axis=0, keepdims=True)
        turned = pltpu.roll(jnp.broadcast_to(mine, (8, 128)), lax.rem(128 - DATE_DEV * me, 128), 1)
        disp_out[a] = turned[0:1, :DATE_DEV]

    for k in range(1, ROW):
        row_copy(k).wait_send()
        mrow_copy(k).wait_send()
    for k in range(1, NZ):
        zsec_copy(k).wait_send()
        mall_copy(k).wait_send()
    for s in (1, 2, 3, 4):
        for c in range(CHUNKS):
            if goes_plus(s, c):
                plus_copy(s, c).wait_send()
            if goes_minus(s, c):
                minus_copy(s, c).wait_send()
    for g in range(len(GROUPS)):
        for k in range(1, ROW):
            x_copy(g, k).wait_send()
    for n, side in ((0, 0), (0, 1), (0, 2), (0, 3), (1, 0), (1, 1)):
        halo_copy(n, side).wait_send()


def per_device(chips, pair_target, pair_slot, offset_fix):
    flat = chips.reshape(DATE_DEV, CHIP * CHIP)
    target = pair_target.reshape(1, PAIRS)
    slot = pair_slot.reshape(1, PAIRS)
    offs = jnp.transpose(offset_fix.reshape(PAIRS, 2), (1, 0))
    vmem = pl.BlockSpec(memory_space=pltpu.VMEM)
    anywhere = pl.BlockSpec(memory_space=pltpu.HBM)
    dma = pltpu.SemaphoreType.DMA
    measure, disp = pl.pallas_call(
        kernel,
        out_shape=(
            jax.ShapeDtypeStruct((3, 1, PAIRS), F32),
            jax.ShapeDtypeStruct((2, 1, DATE_DEV), F32),
        ),
        in_specs=[anywhere] * 4,
        out_specs=(vmem, vmem),
        scratch_shapes=[
            pltpu.VMEM((DATE_DEV, CHIP * CHIP), BF16),
            pltpu.VMEM((1, PAIRS), jnp.int32),
            pltpu.VMEM((1, PAIRS), jnp.int32),
            pltpu.SMEM((2, PAIRS), jnp.int32),
            pltpu.VMEM((2, PAIRS), jnp.int32),
            pltpu.VMEM((DATE_DEV * 32 + 32, 128), F32),
            *[pltpu.VMEM((DATE_DEV, 32, 128), BF16)] * NZ,
            pltpu.VMEM((ROW, NZ, 2, 32, 128), BF16),
            pltpu.VMEM((NZ, ROW, 2, 32, 128), BF16),
            pltpu.VMEM((DATE_DEV, 8, 128), F32),
            pltpu.VMEM((ROW * 16 + 8, 128), F32),
            pltpu.VMEM((NZ * 8 + 8, 128), F32),
            pltpu.VMEM((16, 128), jnp.int32),
            pltpu.SMEM((16, 128), jnp.int32),
            pltpu.VMEM((PAIRS, 32, 384), BF16),
            pltpu.VMEM((PAIRS, 96, 128), BF16),
            pltpu.VMEM((LINKS * NZ * 128, 128), BF16),
            pltpu.VMEM((LINKS * NZ * 8, 128), F32),
            pltpu.VMEM((SLOTS, 128), F32),
            pltpu.VMEM((ROW * 16, 128), F32),
            pltpu.VMEM((NZ * 16 + 16, 128), F32),
            pltpu.VMEM((48, LINKS * NZ * 128), BF16),
            pltpu.VMEM((40, 128), F32),
            pltpu.VMEM((4, 40, 128), F32),
            dma((5,)),
            dma,
            dma((ROW,)),
            dma((ROW,)),
            dma((NZ,)),
            dma((NZ,)),
            dma((4, CHUNKS)),
            dma((4, CHUNKS)),
            dma((4, CHUNKS)),
            dma((4, CHUNKS)),
            dma((len(GROUPS), ROW)),
            dma((len(GROUPS), ROW)),
            dma((ROW,)),
            dma((ROW,)),
            dma((NZ,)),
            dma((NZ,)),
            dma((2, 4)),
            dma((2, 4)),
        ],
        compiler_params=pltpu.CompilerParams(
            collective_id=0, has_side_effects=True, vmem_limit_bytes=40 * 1024 * 1024
        ),
        name="offset_network",
    )(*[pltpu.with_memory_space_constraint(v, pltpu.HBM) for v in (flat, target, slot, offs)])
    return (jnp.transpose(disp, (0, 2, 1)), jnp.transpose(measure, (0, 2, 1)))


def solution(mesh):
    in_specs = (P("date", "space", None), P("date", None), P("date"), P("date", "space", None))
    out_specs = (P(None, "date", "space"), P(None, "date", "space"))
    return jax.shard_map(
        per_device, mesh=mesh, in_specs=in_specs, out_specs=out_specs, check_vma=False
    )
```

```python
import jax
import jax.numpy as jnp
from jax import lax
from jax.experimental import pallas as pl
from jax.experimental.pallas import tpu as pltpu
from jax.sharding import PartitionSpec as P

CHIP = 64
LINKS = 4
ROW = 8
FAR_FIRST = (4, 3, 5, 2, 6, 1, 7)
NZ = 8
DATE_DEV = 16
PAIRS = 64
CHUNKS = 4
CHUNK = DATE_DEV // CHUNKS
SIGMA = 0.6
ZSCALE = 0.5
EPS = 1e-06
LAMBDA = 2.0
MUS = (4.0, 2.0, 1.0)
FIXED = 32.0
ITEMS = 10
F32 = jnp.float32
BF16 = jnp.bfloat16
PRE = (9, 2, 2, 3, 0)
SLOTS = 128
GROUPS = ((0,), (1, 2), (3, 4), (5, 6), (7,))


def iota(shape, dim):
    return lax.broadcasted_iota(jnp.int32, shape, dim)


def fold(rows):
    return jnp.sum(rows.reshape(rows.shape[0] // 8, 8, 128), axis=0)


def thirds_dot(value, chosen):
    first = value.astype(BF16)
    rest = value - first.astype(F32)
    second = rest.astype(BF16)
    third = (rest - second.astype(F32)).astype(BF16)
    out = jnp.dot(jnp.concatenate([first, second, third], axis=0), chosen, preferred_element_type=F32)
    n = value.shape[0]
    return out[:n] + out[n : 2 * n] + out[2 * n :]


def kernel(
    chips_in,
    target_in,
    slot_in,
    offs_in,
    measure_out,
    disp_out,
    chips,
    target,
    slot,
    offs_s,
    offs_v,
    tmp,
    held0,
    held1,
    held2,
    held3,
    held4,
    held5,
    held6,
    held7,
    xsend,
    recv,
    bnorm,
    rowx,
    zsec,
    reqv,
    req,
    mbuf,
    lhs,
    onehot,
    member,
    sums,
    mrow,
    mall,
    spread,
    fsend,
    halo,
    sem_in,
    sem_req,
    row_s,
    row_r,
    zsec_s,
    zsec_r,
    plus_s,
    plus_r,
    minus_s,
    minus_r,
    x_s,
    x_r,
    mrow_s,
    mrow_r,
    mall_s,
    mall_r,
    halo_s,
    halo_r,
):
    held = (held0, held1, held2, held3, held4, held5, held6, held7)
    date = lax.axis_index("date")
    y = lax.axis_index("space")
    ny = lax.axis_size("space")
    mz = lax.div(date, ROW)
    me = lax.rem(date, ROW)

    def row_peer(k):
        return {"date": mz * ROW + lax.rem(me + k, ROW)}

    def z_peer(k):
        return {"date": lax.rem(mz + k, NZ) * ROW + me}

    def y_peer(k):
        return {"space": lax.rem(y + k, ny)}

    def remote(src, dst, ssem, rsem, peer):
        return pltpu.make_async_remote_copy(
            src_ref=src,
            dst_ref=dst,
            send_sem=ssem,
            recv_sem=rsem,
            device_id=peer,
            device_id_type=pl.DeviceIdType.MESH,
        )

    barrier = pltpu.get_barrier_semaphore()
    for k in range(1, ROW):
        pl.semaphore_signal(barrier, inc=1, device_id=row_peer(k), device_id_type=pl.DeviceIdType.MESH)
    for k in range(1, NZ):
        pl.semaphore_signal(barrier, inc=1, device_id=z_peer(k), device_id_type=pl.DeviceIdType.MESH)
    for k in (1, 2, ny - 2, ny - 1):
        pl.semaphore_signal(barrier, inc=1, device_id=y_peer(k), device_id_type=pl.DeviceIdType.MESH)

    loads = [
        pltpu.make_async_copy(src, dst, sem_in.at[n])
        for n, (src, dst) in enumerate(
            ((chips_in, chips), (target_in, target), (slot_in, slot), (offs_in, offs_s), (offs_in, offs_v))
        )
    ]
    for load in loads:
        load.start()
    for load in loads[1:]:
        load.wait()

    sub = iota((PAIRS, 128), 0)
    lane = iota((PAIRS, 128), 1)
    zeros64 = jnp.zeros((1, 128 - PAIRS), jnp.int32)
    trow = jnp.concatenate([target[...], zeros64 - 1], axis=1).astype(F32)
    srow = jnp.concatenate([slot[...], zeros64], axis=1).astype(F32)
    tb = jnp.broadcast_to(trow, (PAIRS, 128))
    sb = jnp.broadcast_to(srow, (PAIRS, 128))
    eye = sub == lane
    tcol = jnp.sum(jnp.where(eye, tb, 0.0), axis=1, keepdims=True)
    scol = jnp.sum(jnp.where(eye, sb, 0.0), axis=1, keepdims=True)
    twin = jnp.where((tcol == tb) & (lane < sub), 1.0, 0.0)
    rank = jnp.sum(twin, axis=1, keepdims=True).astype(jnp.int32)
    holder = tcol.astype(jnp.int32)
    away = (holder // ROW - mz + NZ) % NZ
    turn = jnp.where(away < NZ // 2, 2 * away, 2 * NZ - 1 - 2 * away)
    place = turn * (2 * ROW) + (holder % ROW) * 2 + rank
    wanted = jnp.sum(jnp.where(lane == place, scol, 0.0), axis=0, keepdims=True)
    pair_of = jnp.sum(jnp.where(lane == place, sub.astype(F32), 0.0), axis=0, keepdims=True)
    place_row = jnp.sum(jnp.where(eye, place.astype(F32), 0.0), axis=0, keepdims=True)
    deal = jnp.where(lane == me * DATE_DEV + sub // LINKS, 1.0, 0.0).astype(BF16)
    r8 = iota((8, PAIRS), 0)
    l8 = iota((8, PAIRS), 1)
    ours = (l8 % LINKS) == (r8 % LINKS)
    named = jnp.where(r8 < 4, jnp.broadcast_to(trow[:, :PAIRS], (8, PAIRS)), jnp.broadcast_to(srow[:, :PAIRS], (8, PAIRS)))
    named = jnp.where(ours, named, 0.0).astype(BF16)
    rowx[pl.ds(0, 8), :] = jnp.dot(named, deal, preferred_element_type=F32)
    rowx[pl.ds(8, 8), :] = jnp.broadcast_to(wanted, (8, 128))

    loads[0].wait()
    for j in range(32):
        tmp[pl.ds(j, DATE_DEV, stride=32), :] = chips[:, 128 * j : 128 * j + 128].astype(F32)
    for d in range(DATE_DEV):
        own = tmp[pl.ds(32 * d, 32), :]
        held[0][d] = own.astype(BF16)
        bnorm[d] = fold(own * own)

    pl.semaphore_wait(barrier, ROW - 1 + NZ - 1 + 4)

    def row_copy(k):
        return remote(rowx.at[pl.ds(0, 16)], rowx.at[pl.ds(16 * k, 16)], row_s.at[k], row_r.at[k], row_peer(k))

    def ring_part(t, c):
        return held[t].at[pl.ds(c * CHUNK, CHUNK)]

    def plus_copy(s, c):
        return remote(
            ring_part(max(2 * s - 3, 0), c),
            ring_part(2 * s - 1, c),
            plus_s.at[s - 1, c],
            plus_r.at[s - 1, c],
            z_peer(1),
        )

    def minus_copy(s, c):
        return remote(
            ring_part(2 * s - 2, c),
            ring_part(min(2 * s, 7), c),
            minus_s.at[s - 1, c],
            minus_r.at[s - 1, c],
            z_peer(NZ - 1),
        )

    def goes_plus(s, c):
        return s < 4 or c < CHUNKS // 2

    def goes_minus(s, c):
        return s < 4 or c >= CHUNKS // 2

    for c in range(CHUNKS):
        plus_copy(1, c).start()
        minus_copy(1, c).start()
        if c == 0:
            for k in FAR_FIRST:
                row_copy(k).start()

    lane64 = iota((CHIP, 128), 1)
    spacing_x = ((lane64 % CHIP) - iota((CHIP, 128), 0)).astype(F32)
    left64 = lane64 < CHIP
    lane32 = iota((32, 128), 1)
    q32 = lane32 % CHIP
    m32 = 2 * (q32 % 32) + q32 // 32
    spacing_y = (m32 - 2 * iota((32, 128), 0) - lane32 // CHIP).astype(F32)
    left32 = lane32 < CHIP
    decay = -1.0 / (2.0 * SIGMA * SIGMA)

    def prepare(d, carry):
        own = held[0][d]
        for l in range(LINKS):
            i = d * LINKS + l
            off_y = offs_s[0, i].astype(F32) * (1.0 / FIXED)
            off_x = offs_s[1, i].astype(F32) * (1.0 / FIXED)
            tops, bottoms = [], []
            for level in (-1.0, 0.0, 1.0):
                gap = spacing_x - (off_x + level)
                bell = jnp.exp(gap * gap * decay)
                tops.append(jnp.where(left64, bell, 0.0).astype(BF16))
                bottoms.append(jnp.where(left64, 0.0, bell).astype(BF16))
            wide = jnp.concatenate([jnp.concatenate(tops, axis=1), jnp.concatenate(bottoms, axis=1)], axis=0)
            mbuf[i] = jnp.dot(own, wide, preferred_element_type=F32).astype(BF16)
            for e, level in enumerate((-1.0, 0.0, 1.0)):
                gap = spacing_y - (off_y + level)
                lhs[i, pl.ds(32 * e, 32), :] = jnp.exp(gap * gap * decay).astype(BF16)
        return carry

    def prepare_part(n):
        low = sum(PRE[:n])
        lax.fori_loop(low, low + PRE[n], prepare, 0)

    def forward(s, chunks):
        for c in chunks:
            plus_copy(s, c).wait_recv()
            if goes_plus(s + 1, c):
                plus_copy(s + 1, c).start()
            minus_copy(s, c).wait_recv()
            if goes_minus(s + 1, c):
                minus_copy(s + 1, c).start()

    prepare_part(0)
    forward(1, range(2))
    for k in range(1, ROW):
        row_copy(k).wait_recv()
    reqv[pl.ds(0, 8), :] = rowx[pl.ds(8, 8, stride=16), :].astype(jnp.int32)
    reqv[pl.ds(8, 8), :] = jnp.broadcast_to(pair_of, (8, 128)).astype(jnp.int32)
    fetch = pltpu.make_async_copy(reqv, req, sem_req)
    fetch.start()
    forward(1, range(2, CHUNKS))
    fetch.wait()
    total = rowx[pl.ds(0, 8), :]
    for k in range(1, ROW):
        total = total + rowx[pl.ds(16 * k, 8), :]
    zsec[pl.ds(8 * mz, 8), :] = total

    def zsec_copy(k):
        mine = zsec.at[pl.ds(8 * mz, 8)]
        return remote(mine, mine, zsec_s.at[k], zsec_r.at[k], z_peer(k))

    def zsec_arrived(k):
        theirs = zsec.at[pl.ds(8 * lax.rem(mz - k + NZ, NZ), 8)]
        remote(theirs, theirs, zsec_s.at[k], zsec_r.at[k], z_peer(k)).wait_recv()

    def x_copy(g, k):
        first, count = GROUPS[g][0], len(GROUPS[g])
        return remote(
            xsend.at[k, pl.ds(first, count)],
            recv.at[pl.ds(first, count), me],
            x_s.at[g, k],
            x_r.at[g, k],
            row_peer(k),
        )

    def x_arrived(g, k):
        first, count = GROUPS[g][0], len(GROUPS[g])
        theirs = recv.at[pl.ds(first, count), lax.rem(me - k + ROW, ROW)]
        remote(xsend.at[k, pl.ds(first, count)], theirs, x_s.at[g, k], x_r.at[g, k], row_peer(k)).wait_recv()

    def serve(g):
        for k in (4, 3, 5, 2, 6, 1, 7, 0):
            asker = (ROW - k) % ROW
            for t in GROUPS[g]:
                for r in (0, 1):
                    chip = held[t][jnp.clip(req[asker, t * 2 * ROW + me * 2 + r], 0, DATE_DEV - 1)]
                    if k:
                        xsend[k, t, r] = chip
                    else:
                        recv[t, me, r] = chip
            if k:
                x_copy(g, k).start()

    on_left = jnp.where(left32, 1.0, 0.0).astype(BF16)
    on_right = jnp.where(left32, 0.0, 1.0).astype(BF16)
    sub8 = iota((8, 128), 0)
    lane8 = iota((8, 128), 1)

    def fold8(parts):
        once = [
            jnp.where(sub8 < 4, parts[j], parts[j + 4])
            + pltpu.roll(jnp.where(sub8 < 4, parts[j + 4], parts[j]), 4, 0)
            for j in range(4)
        ]

        def pair(a, b, n):
            return jnp.where(sub8 % (2 * n) < n, a + pltpu.roll(a, 8 - n, 0), b + pltpu.roll(b, n, 0))

        return pair(pair(once[0], once[2], 2), pair(once[1], once[3], 2), 1)

    def score(t, part):
        slots = [t * 2 * ROW + part * 8 + j for j in range(8)]
        pairs = [jnp.clip(req[8, slot], 0, PAIRS - 1) for slot in slots]
        chip = [recv[t, part * 4 + j // 2, j % 2].astype(F32) for j in range(8)]
        lifted = []
        for j in range(8):
            swapped = pltpu.roll(chip[j], CHIP, 1).astype(BF16)
            straight = chip[j].astype(BF16)
            blocks = jnp.concatenate(
                [straight * on_left, swapped * on_left, swapped * on_right, straight * on_right], axis=0
            )
            lifted.append(jnp.dot(lhs[pairs[j]], blocks, preferred_element_type=F32).astype(BF16))
        items = [[] for _ in range(ITEMS)]
        for j in range(8):
            up = lifted[j].astype(F32)
            moved = mbuf[pairs[j]].astype(F32)
            for ky in range(3):
                for kx in range(3):
                    items[3 * ky + kx].append(fold(up[32 * ky : 32 * ky + 32] * moved[:, 128 * kx : 128 * kx + 128]))
            items[9].append(fold(chip[j] * chip[j]))
        table = jnp.zeros((8, 128), F32)
        for item in range(ITEMS):
            table = jnp.where(lane8 == item, jnp.sum(fold8(items[item]), axis=1, keepdims=True), table)
        sums[pl.ds(pl.multiple_of(t * 2 * ROW + part * 8, 8), 8), :] = table

    def score_group(g):
        for k in range(1, ROW):
            x_arrived(g, k)
        for t in GROUPS[g]:
            score(t, 0)
            score(t, 1)

    serve(0)
    serve(1)
    prepare_part(1)
    for s in (2, 3):
        forward(s, range(CHUNKS))
        serve(s)
        prepare_part(s)
    for c in range(CHUNKS):
        (plus_copy if goes_plus(4, c) else minus_copy)(4, c).wait_recv()
    serve(4)
    for k in FAR_FIRST:
        zsec_copy(k).start()
    prepare_part(4)

    for g in range(len(GROUPS)):
        score_group(g)

    chosen = jnp.where(iota((SLOTS, 128), 0).astype(F32) == place_row, 1.0, 0.0).astype(BF16)
    rows = thirds_dot(sums[...].T[:16], chosen)[:, :PAIRS]
    rows = [rows[item : item + 1, :] for item in range(ITEMS)]
    norms = jnp.concatenate([fold8([bnorm[8 * h + j] for j in range(8)]) for h in (0, 1)], axis=0)
    norms = jnp.sum(norms, axis=1, keepdims=True)
    leads = iota((DATE_DEV, PAIRS), 0) == iota((DATE_DEV, PAIRS), 1) // LINKS
    rows.append(jnp.sum(jnp.where(leads, norms, 0.0), axis=0, keepdims=True))
    size = CHIP / jnp.sqrt((rows[10] + EPS) * (rows[9] + EPS))
    scores = [rows[q] * size for q in range(9)]
    raised = [jnp.exp(ZSCALE * s) for s in scores]
    whole = raised[0]
    for q in range(1, 9):
        whole = whole + raised[q]
    weights = [r / whole for r in raised]
    shift_y = (weights[6] + weights[7] + weights[8]) - (weights[0] + weights[1] + weights[2])
    shift_x = (weights[2] + weights[5] + weights[8]) - (weights[0] + weights[3] + weights[6])
    blend = weights[0] * scores[0]
    for q in range(1, 9):
        blend = blend + weights[q] * scores[q]
    quality = 1.0 / (1.0 + jnp.exp(-ZSCALE * blend))
    offs = offs_v[...].astype(F32) * (1.0 / FIXED)
    move_y = offs[0:1] + shift_y
    move_x = offs[1:2] + shift_x
    measure_out[0] = move_y
    measure_out[1] = move_x
    measure_out[2] = quality

    up = jnp.where(r8 < 4, jnp.broadcast_to(move_y, (8, PAIRS)), jnp.broadcast_to(move_x, (8, PAIRS)))
    up = jnp.where(ours, up, 0.0)
    down = jnp.where(ours & (r8 < 4), jnp.broadcast_to(quality, (8, PAIRS)), 0.0)
    both = jnp.concatenate([up, down], axis=0)
    mrow[pl.ds(0, 16), :] = thirds_dot(both, deal)

    def mrow_copy(k):
        return remote(mrow.at[pl.ds(0, 16)], mrow.at[pl.ds(16 * k, 16)], mrow_s.at[k], mrow_r.at[k], row_peer(k))

    for k in FAR_FIRST:
        mrow_copy(k).start()
    for k in range(1, NZ):
        zsec_arrived(k)

    later = []
    for l in range(LINKS):
        dev = zsec[pl.ds(l, NZ, stride=8), :].astype(jnp.int32)
        pos = zsec[pl.ds(4 + l, NZ, stride=8), :].astype(jnp.int32)
        later.append((dev // ROW, (dev % ROW) * DATE_DEV + pos))
    across = iota((128, 128), 1).astype(F32)
    down8 = iota((8, 128), 0)
    for l in range(LINKS):
        columns = later[l][1].astype(F32).T
        for z in range(NZ):
            c = l * NZ + z
            hit = columns[:, z : z + 1] == across
            onehot[pl.ds(128 * c, 128), :] = jnp.where(hit, 1.0, 0.0).astype(BF16)
            hit = jnp.broadcast_to(later[l][0][z : z + 1, :], (8, 128)) == down8
            member[pl.ds(8 * c, 8), :] = jnp.where(hit, 1.0, 0.0)
    for k in range(1, ROW):
        mrow_copy(k).wait_recv()
    total = mrow[pl.ds(0, 16), :]
    for k in range(1, ROW):
        total = total + mrow[pl.ds(16 * k, 16), :]
    mall[pl.ds(16 * mz, 16), :] = total

    def mall_copy(k):
        mine = mall.at[pl.ds(16 * mz, 16)]
        return remote(mine, mine, mall_s.at[k], mall_r.at[k], z_peer(k))

    def mall_arrived(k):
        theirs = mall.at[pl.ds(16 * lax.rem(mz - k + NZ, NZ), 16)]
        remote(theirs, theirs, mall_s.at[k], mall_r.at[k], z_peer(k)).wait_recv()

    for k in FAR_FIRST:
        mall_copy(k).start()
    for k in range(1, NZ):
        mall_arrived(k)

    meas = [[mall[pl.ds(4 * a + l, NZ, stride=16), :] for l in range(LINKS)] for a in range(2)]
    qual = [mall[pl.ds(8 + l, NZ, stride=16), :] for l in range(LINKS)]
    field = None

    def halo_copy(n, side):
        peer = y_peer((1, ny - 1, 2, ny - 2)[side])
        if n == 0:
            return remote(fsend.at[pl.ds(0, 16)], halo.at[side, pl.ds(0, 16)], halo_s.at[0, side], halo_r.at[0, side], peer)
        return remote(fsend.at[pl.ds(16, 24)], halo.at[side, pl.ds(16, 24)], halo_s.at[1, side], halo_r.at[1, side], peer)

    def inside(steps, value):
        return jnp.where((y + steps >= 0) & (y + steps < ny), value, 0.0)

    def settle(beside, numer, denom):
        return [(LAMBDA * beside[a] + numer[a]) / (2.0 * LAMBDA + denom) for a in range(2)]

    for n, scale in enumerate(MUS):
        square = scale * scale
        numer = [None, None]
        denom = None
        for l in range(LINKS):
            if field is None:
                here = [0.0, 0.0]
                there = [0.0, 0.0]
            else:
                here = field
                there = []
                for a in range(2):
                    got = None
                    for z in range(NZ):
                        table = jnp.broadcast_to(field[a][z : z + 1, :], (NZ, 128))
                        found = jnp.take_along_axis(table, later[l][1], axis=1, mode="promise_in_bounds")
                        got = found if got is None else jnp.where(later[l][0] == z, found, got)
                    there.append(got)
            resid = [meas[a][l] - (there[a] - here[a]) for a in range(2)]
            gnc = qual[l] * square / (square + (resid[0] * resid[0] + resid[1] * resid[1]))
            values = [gnc * (here[a] + meas[a][l]) for a in range(2)] + [gnc]
            for a in range(2):
                back = gnc * (there[a] - meas[a][l])
                numer[a] = back if l == 0 else numer[a] + back
            denom = gnc if l == 0 else denom + gnc
            for z in range(NZ):
                c = l * NZ + z
                mask = member[pl.ds(8 * c, 8), :]
                tall = jnp.concatenate(
                    [jnp.broadcast_to(v[z : z + 1, :], (8, 128)) * mask for v in values], axis=0
                )
                high = tall.astype(BF16)
                low = (tall - high.astype(F32)).astype(BF16)
                spread[:, pl.ds(128 * c, 128)] = jnp.concatenate([high, low], axis=0)
        sent = lax.dot_general(
            spread[...], onehot[...], (((1,), (0,)), ((), ())), preferred_element_type=F32
        )
        sent = sent[0:24] + sent[24:48]
        numer = [numer[a] + sent[8 * a : 8 * a + 8] for a in range(2)]
        denom = denom + sent[16:24]
        if n == 0:
            field = [numer[a] / (2.0 * LAMBDA + denom) for a in range(2)]
            for a in range(2):
                fsend[pl.ds(8 * a, 8), :] = field[a]
            for side in range(4):
                halo_copy(0, side).start()
        elif n == 1:
            for a in range(2):
                fsend[pl.ds(16 + 8 * a, 8), :] = numer[a]
            fsend[pl.ds(32, 8), :] = denom
            for side in (0, 1):
                halo_copy(1, side).start()
            for side in (0, 1):
                halo_copy(0, side).wait_recv()
            near = [inside(-1, halo[0, pl.ds(8 * a, 8), :]) + inside(1, halo[1, pl.ds(8 * a, 8), :]) for a in range(2)]
            start = field
            field = settle(near, numer, denom)
        else:
            for side in (2, 3):
                halo_copy(0, side).wait_recv()
            for side in (0, 1):
                halo_copy(1, side).wait_recv()
            beside = [0.0, 0.0]
            for side, way in ((0, -1), (1, 1)):
                reach = [start[a] + inside(2 * way, halo[2 + side, pl.ds(8 * a, 8), :]) for a in range(2)]
                theirs = [halo[side, pl.ds(16 + 8 * a, 8), :] for a in range(2)]
                there = settle(reach, theirs, halo[side, pl.ds(32, 8), :])
                beside = [beside[a] + inside(way, there[a]) for a in range(2)]
            field = settle(beside, numer, denom)

    for a in range(2):
        mine = jnp.sum(jnp.where(down8 == mz, field[a], 0.0), axis=0, keepdims=True)
        turned = pltpu.roll(jnp.broadcast_to(mine, (8, 128)), lax.rem(128 - DATE_DEV * me, 128), 1)
        disp_out[a] = turned[0:1, :DATE_DEV]

    for k in range(1, ROW):
        row_copy(k).wait_send()
        mrow_copy(k).wait_send()
    for k in range(1, NZ):
        zsec_copy(k).wait_send()
        mall_copy(k).wait_send()
    for s in (1, 2, 3, 4):
        for c in range(CHUNKS):
            if goes_plus(s, c):
                plus_copy(s, c).wait_send()
            if goes_minus(s, c):
                minus_copy(s, c).wait_send()
    for g in range(len(GROUPS)):
        for k in range(1, ROW):
            x_copy(g, k).wait_send()
    for n, side in ((0, 0), (0, 1), (0, 2), (0, 3), (1, 0), (1, 1)):
        halo_copy(n, side).wait_send()


def per_device(chips, pair_target, pair_slot, offset_fix):
    flat = chips.reshape(DATE_DEV, CHIP * CHIP)
    target = pair_target.reshape(1, PAIRS)
    slot = pair_slot.reshape(1, PAIRS)
    offs = jnp.transpose(offset_fix.reshape(PAIRS, 2), (1, 0))
    vmem = pl.BlockSpec(memory_space=pltpu.VMEM)
    anywhere = pl.BlockSpec(memory_space=pltpu.HBM)
    dma = pltpu.SemaphoreType.DMA
    measure, disp = pl.pallas_call(
        kernel,
        out_shape=(
            jax.ShapeDtypeStruct((3, 1, PAIRS), F32),
            jax.ShapeDtypeStruct((2, 1, DATE_DEV), F32),
        ),
        in_specs=[anywhere] * 4,
        out_specs=(vmem, vmem),
        scratch_shapes=[
            pltpu.VMEM((DATE_DEV, CHIP * CHIP), BF16),
            pltpu.VMEM((1, PAIRS), jnp.int32),
            pltpu.VMEM((1, PAIRS), jnp.int32),
            pltpu.SMEM((2, PAIRS), jnp.int32),
            pltpu.VMEM((2, PAIRS), jnp.int32),
            pltpu.VMEM((DATE_DEV * 32 + 32, 128), F32),
            *[pltpu.VMEM((DATE_DEV, 32, 128), BF16)] * NZ,
            pltpu.VMEM((ROW, NZ, 2, 32, 128), BF16),
            pltpu.VMEM((NZ, ROW, 2, 32, 128), BF16),
            pltpu.VMEM((DATE_DEV, 8, 128), F32),
            pltpu.VMEM((ROW * 16 + 8, 128), F32),
            pltpu.VMEM((NZ * 8 + 8, 128), F32),
            pltpu.VMEM((16, 128), jnp.int32),
            pltpu.SMEM((16, 128), jnp.int32),
            pltpu.VMEM((PAIRS, 32, 384), BF16),
            pltpu.VMEM((PAIRS, 96, 128), BF16),
            pltpu.VMEM((LINKS * NZ * 128, 128), BF16),
            pltpu.VMEM((LINKS * NZ * 8, 128), F32),
            pltpu.VMEM((SLOTS, 128), F32),
            pltpu.VMEM((ROW * 16, 128), F32),
            pltpu.VMEM((NZ * 16 + 16, 128), F32),
            pltpu.VMEM((48, LINKS * NZ * 128), BF16),
            pltpu.VMEM((40, 128), F32),
            pltpu.VMEM((4, 40, 128), F32),
            dma((5,)),
            dma,
            dma((ROW,)),
            dma((ROW,)),
            dma((NZ,)),
            dma((NZ,)),
            dma((4, CHUNKS)),
            dma((4, CHUNKS)),
            dma((4, CHUNKS)),
            dma((4, CHUNKS)),
            dma((len(GROUPS), ROW)),
            dma((len(GROUPS), ROW)),
            dma((ROW,)),
            dma((ROW,)),
            dma((NZ,)),
            dma((NZ,)),
            dma((2, 4)),
            dma((2, 4)),
        ],
        compiler_params=pltpu.CompilerParams(
            collective_id=0, has_side_effects=True, vmem_limit_bytes=40 * 1024 * 1024
        ),
        name="offset_network",
    )(*[pltpu.with_memory_space_constraint(v, pltpu.HBM) for v in (flat, target, slot, offs)])
    return (jnp.transpose(disp, (0, 2, 1)), jnp.transpose(measure, (0, 2, 1)))


def solution(mesh):
    in_specs = (P("date", "space", None), P("date", None), P("date"), P("date", "space", None))
    out_specs = (P(None, "date", "space"), P(None, "date", "space"))
    return jax.shard_map(
        per_device, mesh=mesh, in_specs=in_specs, out_specs=out_specs, check_vma=False
    )
```
